256 devices in a mesh: row: 16 (over z, core), col: 16 (over x, y).
Axes of the slice: x: 4, y: 4, z: 8, core: 2. Of those that a mesh axis runs over, the one named last changes fastest.
Arguments:
- queries: bfloat16 [32768, 1024], P(('row', 'col')), may hold values from -45 to 45
- keys: bfloat16 [32768, 1024], P(('row', 'col')), may hold values from -4 to 4
- values: bfloat16 [32768, 1024], P(('row', 'col')), may hold values from -6 to 6
- mid_offsets: int32 [16], replicated, may hold values from 0 to 3
- long_offsets: int32 [16], replicated, may hold values from 0 to 15
- out_weight: bfloat16 [1024, 2048], replicated, may hold values from -0.1875 to 0.1875
Outputs:
- layer_out: bfloat16 [32768, 2048], P(('row', 'col'))
The draws below stay inside these ranges and needn't reach their ends.
All inputs are finite; a program needn't handle non-finite values.
Results may differ from the reference program's by a relative error of at most 0.01.
Values may be sent and summed in bfloat16 or wider, within the bound.
No kernel may reach another device: no remote copies, remote signals or barrier semaphores. Data moves between devices by JAX's collectives and lax.ppermute only.
A program may use at most 128 MiB of HBM per device.

```python
import jax
import jax.numpy as jnp
from jax import lax

D = 2048
HEADS = 16
HD = 64
R_MID = 4
R_LONG = 16
TOKENS = 32768
SHORT = 2048
MID = 8192


def draw_queries(key, part):
    key = jax.random.fold_in(key, 5)
    base_draw = jnp.clip(3.0 * jax.random.normal(key, (TOKENS, HEADS * HD), jnp.float32), -12.0, 12.0)
    return base_draw.astype(jnp.bfloat16)


def draw_keys(key, part):
    key = jax.random.fold_in(key, 9)
    base_draw = jnp.clip(jax.random.normal(key, (TOKENS, HEADS * HD), jnp.float32), -4.0, 4.0)
    return base_draw.astype(jnp.bfloat16)


def set_ends(values, key, low, largest):
    dims = values.shape
    place = [jax.random.randint(jax.random.fold_in(key, axis), (), 0, dims[axis]) for axis in range(len(dims))]
    values = values.at[tuple(place)].set(low)
    longest = dims.index(max(dims))
    place[longest] = (place[longest] + 1) % dims[longest]
    return values.at[tuple(place)].set(largest)


def block_scale(stream_key, shape, cuts, least, top_value):
    level = 1.0
    for axis_at, shards_of in cuts:
        heights = jax.random.uniform(jax.random.fold_in(jax.random.fold_in(stream_key, 6), axis_at), (shards_of,), jnp.float32, least / len(cuts), top_value / len(cuts))
        level = level * jnp.repeat(jnp.exp(heights), shape[axis_at] // shards_of).reshape((-1,) + (1,) * (len(shape) - 1 - axis_at))
    return level


def normal_values(stream_key, extent, spread, bound, cuts=(), dtype=jnp.bfloat16):
    drawn = jax.random.normal(stream_key, extent, jnp.float32) * spread
    if len(cuts) > 0:
        drawn = block_scale(stream_key, extent, cuts, -0.22, 0.18) * drawn
    return jnp.clip(drawn, min=-bound, max=bound).astype(dtype)


def setup_inputs(seed: int = 0) -> dict:
    key_list = jax.random.split(jax.random.key(seed), 7)
    queries = draw_queries(jax.random.fold_in(key_list[6], 71), 0)
    keys = draw_keys(jax.random.fold_in(key_list[6], 71), 0)
    values = normal_values(key_list[2], (TOKENS, HEADS * HD), 1.0, 6.0, ((0, 256),))
    mid_offsets = set_ends(jax.random.randint(key_list[3], (HEADS,), 0, R_MID), jax.random.fold_in(key_list[3], 1), 0, R_MID - 1).astype(jnp.int32)
    long_offsets = set_ends(jax.random.randint(key_list[4], (HEADS,), 0, R_LONG), jax.random.fold_in(key_list[4], 1), 0, R_LONG - 1).astype(jnp.int32)
    out_weight = normal_values(key_list[5], (HEADS * HD, D), (HEADS * HD) ** -0.5, 0.1875)
    return {"queries": queries, "keys": keys, "values": values, "mid_offsets": mid_offsets, "long_offsets": long_offsets, "out_weight": out_weight}


NEGATIVE = -1.0e30


def level_attention(queries, keys, values, offsets, segment, dilation):
    row_count = TOKENS // dilation
    length = segment // dilation
    gather_index = offsets.astype(jnp.int32).reshape(1, 1, HEADS, 1)

    def select_rows(source_data):
        shaped = source_data.reshape(row_count, dilation, HEADS, HD)
        picked = jnp.take_along_axis(shaped, gather_index, axis=1)
        return picked.reshape(row_count, HEADS, HD).transpose(1, 0, 2).astype(jnp.float32)

    visible = jnp.arange(length)[None, :] <= jnp.arange(length)[:, None]

    def one_head(operands):
        query_head, key_head, value_head = operands
        query_head = query_head.reshape(row_count // length, length, HD)
        key_head = key_head.reshape(row_count // length, length, HD)
        value_head = value_head.reshape(row_count // length, length, HD)
        scores = jnp.einsum("sqd,skd->sqk", query_head, key_head, precision=lax.Precision.HIGHEST) * (HD ** -0.5)
        scores = jnp.where(visible, scores, NEGATIVE)
        level_max = jnp.max(scores, axis=-1)
        weights = jnp.where(visible, jnp.exp(scores - level_max[..., None]), 0.0)
        running_sum = jnp.sum(weights, axis=-1)
        rounded = lax.optimization_barrier(weights.astype(jnp.bfloat16)).astype(jnp.float32)
        attended = jnp.einsum("sqk,skd->sqd", rounded, value_head, precision=lax.Precision.HIGHEST) / running_sum[..., None]
        return attended.reshape(row_count, HD), (level_max + jnp.log(running_sum)).reshape(row_count)

    attended, log_total = lax.map(one_head, (select_rows(queries), select_rows(keys), select_rows(values)))
    attended = attended.transpose(1, 0, 2)
    log_total = log_total.transpose(1, 0)
    selected = jnp.arange(dilation)[None, :, None] == offsets.astype(jnp.int32)[None, None, :]
    full_log = jnp.where(selected, log_total[:, None, :], NEGATIVE).reshape(TOKENS, HEADS)
    full_out = jnp.where(selected[..., None], attended[:, None], 0.0).reshape(TOKENS, HEADS, HD)
    return full_out, full_log


def reference(queries, keys, values, mid_offsets, long_offsets, out_weight):
    no_offset = jnp.zeros((HEADS,), jnp.int32)
    results = [
        level_attention(queries, keys, values, no_offset, SHORT, 1),
        level_attention(queries, keys, values, mid_offsets, MID, R_MID),
        level_attention(queries, keys, values, long_offsets, TOKENS, R_LONG),
    ]
    level_max = jnp.maximum(jnp.maximum(results[0][1], results[1][1]), results[2][1])
    numerator = jnp.zeros((TOKENS, HEADS, HD), jnp.float32)
    denominator = jnp.zeros((TOKENS, HEADS), jnp.float32)
    for attended, log_total in results:
        weight = jnp.exp(log_total - level_max)
        numerator = numerator + weight[..., None] * attended
        denominator = denominator + weight
    combined = (numerator / denominator[..., None]).astype(jnp.bfloat16).reshape(TOKENS, HEADS * HD)
    return jnp.dot(combined, out_weight, preferred_element_type=jnp.float32).astype(jnp.bfloat16)
```

```python
import functools

import jax
import jax.numpy as jnp
from jax import lax
from jax.experimental import pallas as pl
from jax.experimental.pallas import tpu as pltpu
from jax.sharding import PartitionSpec as P

R_MID = 4
R_LONG = 16
HEADS = 16
HD = 64
LANES = 128
BLOCK = 128
SEG = 2048
HALF = BLOCK // 2
PACKED = BLOCK + HALF
NOTE = 16
ROWS = 16
MID_ROWS = 4
N_MID = SEG // R_MID
N_LONG = SEG // R_LONG
NEGATIVE = -1e30
SCALE = 0.125 * 1.4426950408889634
VMEM_LIMIT = 20 * 1024 * 1024
VMEM_MOST = 60 * 1024 * 1024

VM = pl.BlockSpec(memory_space=pltpu.VMEM)
HB = pl.BlockSpec(memory_space=pl.ANY)
DMA = pltpu.SemaphoreType.DMA


def call(
    kernel, out_shape, in_specs, scratch=(), flops=0, moved=0, exps=0, out_specs=None, aliases=None, limit=VMEM_LIMIT
):
    return pl.pallas_call(
        kernel,
        out_shape=out_shape,
        in_specs=in_specs,
        out_specs=jax.tree.map(lambda _: VM, out_shape) if out_specs is None else out_specs,
        scratch_shapes=list(scratch),
        input_output_aliases=aliases or {},
        compiler_params=pltpu.CompilerParams(vmem_limit_bytes=limit),
        cost_estimate=pl.CostEstimate(flops=flops, bytes_accessed=moved, transcendentals=exps),
    )


def shape(*dims, dtype=jnp.bfloat16):
    return jax.ShapeDtypeStruct(dims, dtype)


def low_lanes(rows):
    return lax.broadcasted_iota(jnp.int32, (rows, LANES), 1) < HD


def fetch(pairs, sems):
    copies = [pltpu.make_async_copy(src, dst, sems.at[i]) for i, (src, dst) in enumerate(pairs)]
    for copy in copies:
        copy.start()
    return copies


def pack_kernel(
    mid_hbm, long_hbm, q_hbm, k_hbm, v_hbm, out_hbm,
    mid_ref, long_ref, q_ref, k_ref, v_ref, out_ref, at_sems, in_sems, out_sems,
):
    notes = fetch([(mid_hbm, mid_ref), (long_hbm, long_ref)], at_sems)
    chunks = in_sems.shape[0]
    heads = HEADS // chunks
    loads, stores = [], []
    for i in range(chunks):
        cols = pl.ds(i * heads * HD, heads * HD)
        pairs = [(src.at[:, cols], dst.at[:, cols]) for src, dst in ((k_hbm, k_ref), (v_hbm, v_ref), (q_hbm, q_ref))]
        loads.append(fetch(pairs, in_sems.at[i]))
    for copy in notes:
        copy.wait()
    for i in range(chunks):
        for copy in loads[i]:
            copy.wait()
        for head in range(i * heads, i * heads + heads):
            cols = pl.ds(head // 2 * LANES, LANES)
            lanes = slice(head % 2 * HD, head % 2 * HD + HD)
            q = q_ref[:, cols][:, lanes]
            out_ref[head, :BLOCK] = jnp.concatenate([k_ref[:, cols][:, lanes], v_ref[:, cols][:, lanes]], axis=1)
            out_ref[head, BLOCK:PACKED] = jnp.concatenate([q[:HALF], q[HALF:]], axis=1)
            note = jnp.where(low_lanes(NOTE), mid_ref[head].astype(jnp.float32), long_ref[head].astype(jnp.float32))
            out_ref[head, PACKED:] = note.astype(jnp.bfloat16)
        done = pl.ds(i * heads, heads)
        stores.append(pltpu.make_async_copy(out_ref.at[done], out_hbm.at[done], out_sems.at[i]))
        stores[-1].start()
    for copy in stores:
        copy.wait()


def select_kernel(got_ref, kvm_ref, far_ref, qm_ref, ql_ref, at_ref, wide):
    for src in range(HEADS):
        wide[0, pl.ds(src * BLOCK, BLOCK), :] = got_ref[src, :BLOCK].astype(jnp.float32)
        packed = got_ref[src, BLOCK:PACKED].astype(jnp.float32)
        wide[1, pl.ds(src * BLOCK, HALF), :] = packed
        wide[1, pl.ds(src * BLOCK + HALF, HALF), :] = pltpu.roll(packed, HD, 1)
    at_ref[...] = got_ref[0, PACKED:].astype(jnp.float32)
    o_mid, o_long = own_offsets(at_ref)
    kvm_ref[...] = wide[0, pl.ds(o_mid, N_MID, stride=R_MID), :].astype(jnp.bfloat16)
    far = wide[0, pl.ds(o_long, N_LONG, stride=R_LONG), :].astype(jnp.bfloat16)
    for z in range(ROWS // 2):
        far_ref[z] = far
    q = wide[1, pl.ds(o_mid, N_MID, stride=R_MID), :]
    qm_ref[...] = jnp.where(low_lanes(N_MID), q, 0.0).astype(jnp.bfloat16)
    q = wide[1, pl.ds(o_long, N_LONG, stride=R_LONG), :]
    ql_ref[...] = jnp.where(low_lanes(N_LONG), q, 0.0).astype(jnp.bfloat16)


def own_offsets(at_ref):
    lane = lax.broadcasted_iota(jnp.int32, at_ref.shape, 1)
    at = at_ref[...].astype(jnp.int32)
    return [jnp.max(jnp.where(lane == where, at, 0)) for where in (0, LANES - 1)]


def scores_of(q, kv):
    return lax.dot_general(q, kv, (((1,), (1,)), ((), ())), preferred_element_type=jnp.float32)


def with_ones(kv):
    return jnp.where(low_lanes(kv.shape[0]), jnp.ones_like(kv), kv)


def soft(s, kv1):
    top = jnp.max(s, axis=1, keepdims=True)
    w = jnp.exp2((s - top) * SCALE).astype(jnp.bfloat16)
    return top, jnp.dot(w, kv1, preferred_element_type=jnp.float32)


def state_of(top, acc):
    lane = lax.broadcasted_iota(jnp.int32, acc.shape, 1)
    return jnp.where((lane >= HD // 2) & (lane < HD), top, acc)


def merge(state, rows, new_top, new_acc):
    old = state[rows, :]
    old_top = old[:, HD // 2 : HD // 2 + 1]
    best = jnp.maximum(old_top, new_top)
    acc = old * jnp.exp2((old_top - best) * SCALE) + new_acc * jnp.exp2((new_top - best) * SCALE)
    state[rows, :] = state_of(best, acc)


def causal(rows, cols, first):
    at = lax.broadcasted_iota(jnp.int32, (rows, cols), 0) + first
    return lax.broadcasted_iota(jnp.int32, (rows, cols), 1) <= at


def short_kernel(at_ref, got_ref, kvm, far_ref, qm_ref, ql_ref, state, kv_buf, one_buf):
    for src in range(HEADS):
        rows = pl.ds(src * BLOCK, BLOCK)
        kv = got_ref[src, :BLOCK]
        kv_buf[rows, :] = kv
        one_buf[rows, :] = with_ones(kv)
    step = 2 * BLOCK
    visible = causal(step, step, 0)
    low = low_lanes(HALF)
    zero = jnp.zeros((HALF, LANES), jnp.bfloat16)
    for i in range(SEG // step):
        parts = []
        for src in (2 * i, 2 * i + 1):
            packed = got_ref[src, BLOCK:PACKED]
            parts.append(jnp.where(low, packed, zero))
            parts.append(jnp.where(low, jnp.concatenate([packed[:, HD:], packed[:, :HD]], axis=1), zero))
        q = jnp.concatenate(parts, axis=0)
        rows = pl.ds(i * step, step)
        n = (i + 1) * step
        s = scores_of(q, kv_buf[rows, :])
        s = jnp.where(visible, s, NEGATIVE)
        if i:
            s = jnp.concatenate([scores_of(q, kv_buf[pl.ds(0, i * step), :]), s], axis=1)
        state[rows, :] = state_of(*soft(s, one_buf[pl.ds(0, n), :]))
    o_mid, o_long = own_offsets(at_ref)
    for i in range(N_MID // step):
        n = (i + 1) * step
        s = scores_of(qm_ref[pl.ds(i * step, step), :], kvm[:n])
        top, acc = soft(jnp.where(causal(step, n, i * step), s, NEGATIVE), with_ones(kvm[:n]))
        merge(state, pl.ds(o_mid + i * step * R_MID, step, stride=R_MID), top, acc)
    far = far_ref[0]
    s = scores_of(ql_ref[...], far)
    top, acc = soft(jnp.where(causal(N_LONG, N_LONG, 0), s, NEGATIVE), with_ones(far))
    merge(state, pl.ds(o_long, N_LONG, stride=R_LONG), top, acc)


def last_kernel(at_ref, state_in, qm, m1, m2, m3, ql, same, other, w_hbm, out_ref, state, w_ref, w_sem):
    load = pltpu.make_async_copy(w_hbm, w_ref, w_sem)
    load.start()
    o_mid, o_long = own_offsets(at_ref)
    row = lax.axis_index("row")
    pos = lax.rem(row, MID_ROWS)
    step = 256
    for i in range(N_MID // step):
        q = qm[pl.ds(i * step, step), :]
        pieces, ones = [], []
        for d, ref in ((1, m1), (2, m2), (3, m3)):
            before = jnp.bitwise_xor(pos, d) < pos
            pieces.append(scores_of(q, ref[...]) + jnp.where(before, 0.0, NEGATIVE))
            ones.append(with_ones(ref[...]))
        top, new = soft(jnp.concatenate(pieces, axis=1), jnp.concatenate(ones, axis=0))
        merge(state, pl.ds(o_mid + i * step * R_MID, step, stride=R_MID), top, new)
    q = ql[...]
    pieces, ones = [], []
    core = lax.rem(row, 2)
    half = (ROWS // 2) * N_LONG
    for ref, its_core in ((same, core), (other, 1 - core)):
        every = ref[...].reshape(half, LANES)
        s = scores_of(q, every)
        before = lax.broadcasted_iota(jnp.int32, s.shape, 1) < ((row + 1 - its_core) // 2) * N_LONG
        pieces.append(jnp.where(before, s, NEGATIVE))
        ones.append(with_ones(every))
    top, new = soft(jnp.concatenate(pieces, axis=1), jnp.concatenate(ones, axis=0))
    merge(state, pl.ds(o_long, N_LONG, stride=R_LONG), top, new)
    low = low_lanes(HALF)
    for src in range(HEADS):
        done = []
        for half in range(2):
            a = state[pl.ds(src * BLOCK + half * HALF, HALF), :]
            done.append(a / a[:, :1])
        out_ref[src] = jnp.where(low, pltpu.roll(done[0], HD, 1), done[1]).astype(jnp.bfloat16)
    load.wait()


def project_kernel(got_ref, w_ref, out_hbm, combined, tiles, sems):
    count, _, tile = tiles.shape
    for pair in range(HEADS // 2):
        a, b = got_ref[2 * pair], got_ref[2 * pair + 1]
        cols = pl.ds(pair * LANES, LANES)
        combined[:HALF, cols] = jnp.concatenate([a[:, :HD], b[:, :HD]], axis=1)
        combined[HALF:, cols] = jnp.concatenate([a[:, HD:], b[:, HD:]], axis=1)
    rows = combined[...]
    copies = []
    for i in range(count):
        cols = pl.ds(i * tile, tile)
        tiles[i] = jnp.dot(rows, w_ref[:, cols], preferred_element_type=jnp.float32).astype(jnp.bfloat16)
        copies.append(pltpu.make_async_copy(tiles.at[i], out_hbm.at[:, cols], sems.at[i]))
        copies[-1].start()
    for copy in copies:
        copy.wait()


def xor_rows(x, d):
    return lax.ppermute(x, "row", [(i, i ^ d) for i in range(ROWS)])


CORES = [[2 * z + c for z in range(ROWS // 2)] for c in range(2)]
bar = lax.optimization_barrier


def shards(queries, keys, values, mid_offsets, long_offsets, out_weight):
    f32, s32, bf16 = jnp.float32, jnp.int32, jnp.bfloat16
    width = queries.shape[1]
    depth, wide_out = out_weight.shape
    chunks = 4
    sent = call(
        pack_kernel,
        shape(HEADS, PACKED + NOTE, LANES),
        [HB] * 5,
        scratch=[pltpu.SMEM((HEADS,), s32)] * 2
        + [pltpu.VMEM((BLOCK, width), bf16)] * 3
        + [pltpu.VMEM((HEADS, PACKED + NOTE, LANES), bf16), DMA((2,)), DMA((chunks, 3)), DMA((chunks,))],
        moved=1 << 20,
        out_specs=HB,
        limit=VMEM_MOST,
    )(mid_offsets, long_offsets, queries, keys, values)
    got = lax.all_to_all(sent, "col", 0, 0)
    kv_mid, far, q_mid, q_long, at = call(
        select_kernel,
        (
            shape(N_MID, LANES),
            shape(ROWS // 2, N_LONG, LANES),
            shape(N_MID, LANES),
            shape(N_LONG, LANES),
            shape(NOTE, LANES, dtype=f32),
        ),
        [VM],
        scratch=[pltpu.VMEM((2, SEG, LANES), f32)],
        moved=1 << 20,
    )(got)
    m1 = xor_rows(kv_mid, 1)
    m2 = xor_rows(kv_mid, 2)
    same = lax.all_to_all(far, "row", 0, 0, axis_index_groups=CORES)
    state = call(
        short_kernel,
        shape(SEG, LANES, dtype=f32),
        [VM] * 6,
        scratch=[pltpu.VMEM((SEG, LANES), bf16)] * 2,
        flops=4 * SEG * SEG * LANES,
        moved=3 << 20,
        exps=SEG * SEG // 2,
    )(at, got, kv_mid, far, q_mid, q_long)
    same, m2, state = bar((same, m2, state))
    m3 = xor_rows(m2, 1)
    other = xor_rows(same, 1)
    back, _, weight = call(
        last_kernel,
        (shape(HEADS, HALF, LANES), shape(SEG, LANES, dtype=f32), shape(depth, wide_out)),
        [VM] * 9 + [HB],
        scratch=[DMA],
        flops=4 * N_MID * SEG * LANES,
        moved=4 << 20,
        exps=N_MID * SEG,
        aliases={1: 1},
    )(at, state, q_mid, m1, m2, m3, q_long, same, other, out_weight)
    tile = 512
    count = wide_out // tile
    return call(
        project_kernel,
        shape(BLOCK, wide_out),
        [VM, VM],
        scratch=[
            pltpu.VMEM((BLOCK, depth), jnp.bfloat16),
            pltpu.VMEM((count, BLOCK, tile), jnp.bfloat16),
            DMA((count,)),
        ],
        flops=2 * BLOCK * depth * wide_out,
        moved=2 * depth * wide_out,
        out_specs=HB,
    )(lax.all_to_all(back, "col", 0, 0), weight)


def solution(mesh):
    split = P(("row", "col"), None)
    return jax.shard_map(
        shards,
        mesh=mesh,
        in_specs=(split, split, split, P(), P(), P()),
        out_specs=split,
        check_vma=False,
    )
```

```python
import functools

import jax
import jax.numpy as jnp
from jax import lax
from jax.experimental import pallas as pl
from jax.experimental.pallas import tpu as pltpu
from jax.sharding import PartitionSpec as P

R_MID = 4
R_LONG = 16
HEADS = 16
HD = 64
LANES = 128
BLOCK = 128
SEG = 2048
HALF = BLOCK // 2
PACKED = BLOCK + HALF
NOTE = 16
ROWS = 16
MID_ROWS = 4
N_MID = SEG // R_MID
N_LONG = SEG // R_LONG
NEGATIVE = -1e30
SCALE = 0.125 * 1.4426950408889634
VMEM_LIMIT = 20 * 1024 * 1024
VMEM_LAST = 46 * 1024 * 1024
VMEM_MOST = 60 * 1024 * 1024

VM = pl.BlockSpec(memory_space=pltpu.VMEM)
HB = pl.BlockSpec(memory_space=pl.ANY)
DMA = pltpu.SemaphoreType.DMA


def call(
    kernel, out_shape, in_specs, scratch=(), flops=0, moved=0, exps=0, out_specs=None, aliases=None, limit=VMEM_LIMIT
):
    return pl.pallas_call(
        kernel,
        out_shape=out_shape,
        in_specs=in_specs,
        out_specs=jax.tree.map(lambda _: VM, out_shape) if out_specs is None else out_specs,
        scratch_shapes=list(scratch),
        input_output_aliases=aliases or {},
        compiler_params=pltpu.CompilerParams(vmem_limit_bytes=limit),
        cost_estimate=pl.CostEstimate(flops=flops, bytes_accessed=moved, transcendentals=exps),
    )


def shape(*dims, dtype=jnp.bfloat16):
    return jax.ShapeDtypeStruct(dims, dtype)


def low_lanes(rows):
    return lax.broadcasted_iota(jnp.int32, (rows, LANES), 1) < HD


def fetch(pairs, sems):
    copies = [pltpu.make_async_copy(src, dst, sems.at[i]) for i, (src, dst) in enumerate(pairs)]
    for copy in copies:
        copy.start()
    return copies


def pack_kernel(
    mid_hbm, long_hbm, q_hbm, k_hbm, v_hbm, out_hbm,
    mid_ref, long_ref, q_ref, k_ref, v_ref, out_ref, at_sems, in_sems, out_sems,
):
    notes = fetch([(mid_hbm, mid_ref), (long_hbm, long_ref)], at_sems)
    chunks = in_sems.shape[0]
    heads = HEADS // chunks
    loads, stores = [], []
    for i in range(chunks):
        cols = pl.ds(i * heads * HD, heads * HD)
        pairs = [(src.at[:, cols], dst.at[:, cols]) for src, dst in ((k_hbm, k_ref), (v_hbm, v_ref), (q_hbm, q_ref))]
        loads.append(fetch(pairs, in_sems.at[i]))
    for copy in notes:
        copy.wait()
    for i in range(chunks):
        for copy in loads[i]:
            copy.wait()
        for head in range(i * heads, i * heads + heads):
            cols = pl.ds(head // 2 * LANES, LANES)
            lanes = slice(head % 2 * HD, head % 2 * HD + HD)
            q = q_ref[:, cols][:, lanes]
            out_ref[head, :BLOCK] = jnp.concatenate([k_ref[:, cols][:, lanes], v_ref[:, cols][:, lanes]], axis=1)
            out_ref[head, BLOCK:PACKED] = jnp.concatenate([q[:HALF], q[HALF:]], axis=1)
            note = jnp.where(low_lanes(NOTE), mid_ref[head].astype(jnp.float32), long_ref[head].astype(jnp.float32))
            out_ref[head, PACKED:] = note.astype(jnp.bfloat16)
        done = pl.ds(i * heads, heads)
        stores.append(pltpu.make_async_copy(out_ref.at[done], out_hbm.at[done], out_sems.at[i]))
        stores[-1].start()
    for copy in stores:
        copy.wait()


def select_kernel(got_ref, kvm_ref, far_ref, qm_ref, ql_ref, at_ref, wide):
    for src in range(HEADS):
        wide[0, pl.ds(src * BLOCK, BLOCK), :] = got_ref[src, :BLOCK].astype(jnp.float32)
        packed = got_ref[src, BLOCK:PACKED].astype(jnp.float32)
        wide[1, pl.ds(src * BLOCK, HALF), :] = packed
        wide[1, pl.ds(src * BLOCK + HALF, HALF), :] = pltpu.roll(packed, HD, 1)
    at_ref[...] = got_ref[0, PACKED:].astype(jnp.float32)
    o_mid, o_long = own_offsets(at_ref)
    kvm_ref[...] = wide[0, pl.ds(o_mid, N_MID, stride=R_MID), :].astype(jnp.bfloat16)
    far = wide[0, pl.ds(o_long, N_LONG, stride=R_LONG), :].astype(jnp.bfloat16)
    for z in range(ROWS // 2):
        far_ref[z] = far
    q = wide[1, pl.ds(o_mid, N_MID, stride=R_MID), :]
    qm_ref[...] = jnp.where(low_lanes(N_MID), q, 0.0).astype(jnp.bfloat16)
    q = wide[1, pl.ds(o_long, N_LONG, stride=R_LONG), :]
    ql_ref[...] = jnp.where(low_lanes(N_LONG), q, 0.0).astype(jnp.bfloat16)


def own_offsets(at_ref):
    lane = lax.broadcasted_iota(jnp.int32, at_ref.shape, 1)
    at = at_ref[...].astype(jnp.int32)
    return [jnp.max(jnp.where(lane == where, at, 0)) for where in (0, LANES - 1)]


def scores_of(q, kv):
    return lax.dot_general(q, kv, (((1,), (1,)), ((), ())), preferred_element_type=jnp.float32)


def with_ones(kv):
    return jnp.where(low_lanes(kv.shape[0]), jnp.ones_like(kv), kv)


def soft(s, kv1):
    top = jnp.max(s, axis=1, keepdims=True)
    w = jnp.exp2((s - top) * SCALE).astype(jnp.bfloat16)
    return top, jnp.dot(w, kv1, preferred_element_type=jnp.float32)


def state_of(top, acc):
    lane = lax.broadcasted_iota(jnp.int32, acc.shape, 1)
    return jnp.where((lane >= HD // 2) & (lane < HD), top, acc)


def merge(state, rows, new_top, new_acc):
    old = state[rows, :]
    old_top = old[:, HD // 2 : HD // 2 + 1]
    best = jnp.maximum(old_top, new_top)
    acc = old * jnp.exp2((old_top - best) * SCALE) + new_acc * jnp.exp2((new_top - best) * SCALE)
    state[rows, :] = state_of(best, acc)


def causal(rows, cols, first):
    at = lax.broadcasted_iota(jnp.int32, (rows, cols), 0) + first
    return lax.broadcasted_iota(jnp.int32, (rows, cols), 1) <= at


def short_kernel(at_ref, got_ref, kvm, far_ref, qm_ref, ql_ref, state, kv_buf, one_buf):
    for src in range(HEADS):
        rows = pl.ds(src * BLOCK, BLOCK)
        kv = got_ref[src, :BLOCK]
        kv_buf[rows, :] = kv
        one_buf[rows, :] = with_ones(kv)
    step = 2 * BLOCK
    visible = causal(step, step, 0)
    low = low_lanes(HALF)
    zero = jnp.zeros((HALF, LANES), jnp.bfloat16)
    for i in range(SEG // step):
        parts = []
        for src in (2 * i, 2 * i + 1):
            packed = got_ref[src, BLOCK:PACKED]
            parts.append(jnp.where(low, packed, zero))
            parts.append(jnp.where(low, jnp.concatenate([packed[:, HD:], packed[:, :HD]], axis=1), zero))
        q = jnp.concatenate(parts, axis=0)
        rows = pl.ds(i * step, step)
        n = (i + 1) * step
        s = scores_of(q, kv_buf[rows, :])
        s = jnp.where(visible, s, NEGATIVE)
        if i:
            s = jnp.concatenate([scores_of(q, kv_buf[pl.ds(0, i * step), :]), s], axis=1)
        state[rows, :] = state_of(*soft(s, one_buf[pl.ds(0, n), :]))
    o_mid, o_long = own_offsets(at_ref)
    for i in range(N_MID // step):
        n = (i + 1) * step
        s = scores_of(qm_ref[pl.ds(i * step, step), :], kvm[:n])
        top, acc = soft(jnp.where(causal(step, n, i * step), s, NEGATIVE), with_ones(kvm[:n]))
        merge(state, pl.ds(o_mid + i * step * R_MID, step, stride=R_MID), top, acc)
    far = far_ref[0]
    s = scores_of(ql_ref[...], far)
    top, acc = soft(jnp.where(causal(N_LONG, N_LONG, 0), s, NEGATIVE), with_ones(far))
    merge(state, pl.ds(o_long, N_LONG, stride=R_LONG), top, acc)


def mid_part(state, qm, o_mid, pos, parts):
    step = 256
    ones = jnp.concatenate([with_ones(ref[...]) for _, ref in parts], axis=0)
    for i in range(N_MID // step):
        q = qm[pl.ds(i * step, step), :]
        pieces = []
        for d, ref in parts:
            before = jnp.bitwise_xor(pos, d) < pos
            pieces.append(scores_of(q, ref[...]) + jnp.where(before, 0.0, NEGATIVE))
        top, new = soft(jnp.concatenate(pieces, axis=1), ones)
        merge(state, pl.ds(o_mid + i * step * R_MID, step, stride=R_MID), top, new)


def long_part(state, ql, o_long, row, its_core, ref):
    every = ref[...].reshape(ROWS // 2 * N_LONG, LANES)
    s = scores_of(ql[...], every)
    before = lax.broadcasted_iota(jnp.int32, s.shape, 1) < ((row + 1 - its_core) // 2) * N_LONG
    top, new = soft(jnp.where(before, s, NEGATIVE), with_ones(every))
    merge(state, pl.ds(o_long, N_LONG, stride=R_LONG), top, new)


def near_kernel(at_ref, state_in, qm, m1, m2, ql, same, state):
    o_mid, o_long = own_offsets(at_ref)
    row = lax.axis_index("row")
    mid_part(state, qm, o_mid, lax.rem(row, MID_ROWS), ((1, m1), (2, m2)))
    long_part(state, ql, o_long, row, lax.rem(row, 2), same)


def last_kernel(at_ref, state_in, qm, m3, ql, other, w_hbm, out_ref, state, w_ref, w_sem):
    load = pltpu.make_async_copy(w_hbm, w_ref, w_sem)
    load.start()
    o_mid, o_long = own_offsets(at_ref)
    row = lax.axis_index("row")
    mid_part(state, qm, o_mid, lax.rem(row, MID_ROWS), ((3, m3),))
    long_part(state, ql, o_long, row, 1 - lax.rem(row, 2), other)
    low = low_lanes(HALF)
    for src in range(HEADS):
        done = []
        for half in range(2):
            a = state[pl.ds(src * BLOCK + half * HALF, HALF), :]
            done.append(a / a[:, :1])
        out_ref[src] = jnp.where(low, pltpu.roll(done[0], HD, 1), done[1]).astype(jnp.bfloat16)
    load.wait()


def project_kernel(got_ref, w_ref, out_hbm, combined, tiles, sems):
    count, _, tile = tiles.shape
    for pair in range(HEADS // 2):
        a, b = got_ref[2 * pair], got_ref[2 * pair + 1]
        cols = pl.ds(pair * LANES, LANES)
        combined[:HALF, cols] = jnp.concatenate([a[:, :HD], b[:, :HD]], axis=1)
        combined[HALF:, cols] = jnp.concatenate([a[:, HD:], b[:, HD:]], axis=1)
    rows = combined[...]
    copies = []
    for i in range(count):
        cols = pl.ds(i * tile, tile)
        tiles[i] = jnp.dot(rows, w_ref[:, cols], preferred_element_type=jnp.float32).astype(jnp.bfloat16)
        copies.append(pltpu.make_async_copy(tiles.at[i], out_hbm.at[:, cols], sems.at[i]))
        copies[-1].start()
    for copy in copies:
        copy.wait()


def xor_rows(x, d):
    return lax.ppermute(x, "row", [(i, i ^ d) for i in range(ROWS)])


CORES = [[2 * z + c for z in range(ROWS // 2)] for c in range(2)]
bar = lax.optimization_barrier


def shards(queries, keys, values, mid_offsets, long_offsets, out_weight):
    f32, s32, bf16 = jnp.float32, jnp.int32, jnp.bfloat16
    width = queries.shape[1]
    depth, wide_out = out_weight.shape
    chunks = 4
    sent = call(
        pack_kernel,
        shape(HEADS, PACKED + NOTE, LANES),
        [HB] * 5,
        scratch=[pltpu.SMEM((HEADS,), s32)] * 2
        + [pltpu.VMEM((BLOCK, width), bf16)] * 3
        + [pltpu.VMEM((HEADS, PACKED + NOTE, LANES), bf16), DMA((2,)), DMA((chunks, 3)), DMA((chunks,))],
        moved=1 << 20,
        out_specs=HB,
        limit=VMEM_MOST,
    )(mid_offsets, long_offsets, queries, keys, values)
    got = lax.all_to_all(sent, "col", 0, 0)
    kv_mid, far, q_mid, q_long, at = call(
        select_kernel,
        (
            shape(N_MID, LANES),
            shape(ROWS // 2, N_LONG, LANES),
            shape(N_MID, LANES),
            shape(N_LONG, LANES),
            shape(NOTE, LANES, dtype=f32),
        ),
        [VM],
        scratch=[pltpu.VMEM((2, SEG, LANES), f32)],
        moved=1 << 20,
    )(got)
    m1 = xor_rows(kv_mid, 1)
    m2 = xor_rows(kv_mid, 2)
    same = lax.all_to_all(far, "row", 0, 0, axis_index_groups=CORES)
    state = call(
        short_kernel,
        shape(SEG, LANES, dtype=f32),
        [VM] * 6,
        scratch=[pltpu.VMEM((SEG, LANES), bf16)] * 2,
        flops=4 * SEG * SEG * LANES,
        moved=3 << 20,
        exps=SEG * SEG // 2,
    )(at, got, kv_mid, far, q_mid, q_long)
    same, m1, m2, state = bar((same, m1, m2, state))
    m3 = xor_rows(m2, 1)
    other = xor_rows(same, 1)
    state = call(
        near_kernel,
        shape(SEG, LANES, dtype=f32),
        [VM] * 7,
        flops=4 * N_MID * SEG * LANES,
        moved=2 << 20,
        exps=N_MID * SEG,
        aliases={1: 0},
    )(at, state, q_mid, m1, m2, q_long, same)
    back, _, weight = call(
        last_kernel,
        (shape(HEADS, HALF, LANES), shape(SEG, LANES, dtype=f32), shape(depth, wide_out)),
        [VM] * 6 + [HB],
        scratch=[DMA],
        flops=4 * N_MID * SEG * LANES,
        moved=4 << 20,
        exps=N_MID * SEG,
        aliases={1: 1},
        limit=VMEM_LAST,
    )(at, state, q_mid, m3, q_long, other, out_weight)
    tile = 512
    count = wide_out // tile
    return call(
        project_kernel,
        shape(BLOCK, wide_out),
        [VM, VM],
        scratch=[
            pltpu.VMEM((BLOCK, depth), jnp.bfloat16),
            pltpu.VMEM((count, BLOCK, tile), jnp.bfloat16),
            DMA((count,)),
        ],
        flops=2 * BLOCK * depth * wide_out,
        moved=2 * depth * wide_out,
        out_specs=HB,
    )(lax.all_to_all(back, "col", 0, 0), weight)


def solution(mesh):
    split = P(("row", "col"), None)
    return jax.shard_map(
        shards,
        mesh=mesh,
        in_specs=(split, split, split, P(), P(), P()),
        out_specs=split,
        check_vma=False,
    )
```

```python
import functools

import jax
import jax.numpy as jnp
from jax import lax
from jax.experimental import pallas as pl
from jax.experimental.pallas import tpu as pltpu
from jax.sharding import PartitionSpec as P

R_MID = 4
R_LONG = 16
HEADS = 16
HD = 64
LANES = 128
BLOCK = 128
SEG = 2048
HALF = BLOCK // 2
PACKED = BLOCK + HALF
NOTE = 16
ROWS = 16
MID_ROWS = 4
N_MID = SEG // R_MID
N_LONG = SEG // R_LONG
NEGATIVE = -1e30
SCALE = 0.125 * 1.4426950408889634
VMEM_LIMIT = 20 * 1024 * 1024
VMEM_LAST = 47 * 1024 * 1024
VMEM_NEAR = 49 * 1024 * 1024
VMEM_MOST = 60 * 1024 * 1024

VM = pl.BlockSpec(memory_space=pltpu.VMEM)
HB = pl.BlockSpec(memory_space=pl.ANY)
DMA = pltpu.SemaphoreType.DMA


def call(
    kernel, out_shape, in_specs, scratch=(), flops=0, moved=0, exps=0, out_specs=None, aliases=None, limit=VMEM_LIMIT
):
    return pl.pallas_call(
        kernel,
        out_shape=out_shape,
        in_specs=in_specs,
        out_specs=jax.tree.map(lambda _: VM, out_shape) if out_specs is None else out_specs,
        scratch_shapes=list(scratch),
        input_output_aliases=aliases or {},
        compiler_params=pltpu.CompilerParams(vmem_limit_bytes=limit),
        cost_estimate=pl.CostEstimate(flops=flops, bytes_accessed=moved, transcendentals=exps),
    )


def shape(*dims, dtype=jnp.bfloat16):
    return jax.ShapeDtypeStruct(dims, dtype)


def low_lanes(rows):
    return lax.broadcasted_iota(jnp.int32, (rows, LANES), 1) < HD


def fetch(pairs, sems):
    copies = [pltpu.make_async_copy(src, dst, sems.at[i]) for i, (src, dst) in enumerate(pairs)]
    for copy in copies:
        copy.start()
    return copies


def pack_kernel(
    mid_hbm, long_hbm, q_hbm, k_hbm, v_hbm, out_hbm,
    mid_ref, long_ref, q_ref, k_ref, v_ref, out_ref, at_sems, in_sems, out_sems,
):
    notes = fetch([(mid_hbm, mid_ref), (long_hbm, long_ref)], at_sems)
    chunks = in_sems.shape[0]
    heads = HEADS // chunks
    loads, stores = [], []
    for i in range(chunks):
        cols = pl.ds(i * heads * HD, heads * HD)
        pairs = [(src.at[:, cols], dst.at[:, cols]) for src, dst in ((k_hbm, k_ref), (v_hbm, v_ref), (q_hbm, q_ref))]
        loads.append(fetch(pairs, in_sems.at[i]))
    for copy in notes:
        copy.wait()
    for i in range(chunks):
        for copy in loads[i]:
            copy.wait()
        for head in range(i * heads, i * heads + heads):
            cols = pl.ds(head // 2 * LANES, LANES)
            lanes = slice(head % 2 * HD, head % 2 * HD + HD)
            q = q_ref[:, cols][:, lanes]
            out_ref[head, :BLOCK] = jnp.concatenate([k_ref[:, cols][:, lanes], v_ref[:, cols][:, lanes]], axis=1)
            out_ref[head, BLOCK:PACKED] = jnp.concatenate([q[:HALF], q[HALF:]], axis=1)
            note = jnp.where(low_lanes(NOTE), mid_ref[head].astype(jnp.float32), long_ref[head].astype(jnp.float32))
            out_ref[head, PACKED:] = note.astype(jnp.bfloat16)
        done = pl.ds(i * heads, heads)
        stores.append(pltpu.make_async_copy(out_ref.at[done], out_hbm.at[done], out_sems.at[i]))
        stores[-1].start()
    for copy in stores:
        copy.wait()


def select_kernel(got_ref, kvm_ref, own_ref, at_ref, far_ref, wide):
    at_ref[...] = got_ref[0, PACKED:].astype(jnp.float32)
    o_mid, o_long = own_offsets(at_ref)
    for src in range(HEADS):
        wide[pl.ds(src * BLOCK, BLOCK), :] = got_ref[src, :BLOCK].astype(jnp.float32)
    far = wide[pl.ds(o_long, N_LONG, stride=R_LONG), :].astype(jnp.bfloat16)
    own_ref[...] = far
    for z in range(ROWS // 2):
        far_ref[z] = far
    kvm_ref[...] = wide[pl.ds(o_mid, N_MID, stride=R_MID), :].astype(jnp.bfloat16)


def own_offsets(at_ref):
    lane = lax.broadcasted_iota(jnp.int32, at_ref.shape, 1)
    at = at_ref[...].astype(jnp.int32)
    return [jnp.max(jnp.where(lane == where, at, 0)) for where in (0, LANES - 1)]


def scores_of(q, kv):
    return lax.dot_general(q, kv, (((1,), (1,)), ((), ())), preferred_element_type=jnp.float32)


def with_ones(kv):
    return jnp.where(low_lanes(kv.shape[0]), jnp.ones_like(kv), kv)


def soft(s, kv1):
    top = jnp.max(s, axis=1, keepdims=True)
    w = jnp.exp2((s - top) * SCALE).astype(jnp.bfloat16)
    return top, jnp.dot(w, kv1, preferred_element_type=jnp.float32)


def state_of(top, acc):
    lane = lax.broadcasted_iota(jnp.int32, acc.shape, 1)
    return jnp.where((lane >= HD // 2) & (lane < HD), top, acc)


def merge(state, rows, new_top, new_acc):
    old = state[rows, :]
    old_top = old[:, HD // 2 : HD // 2 + 1]
    best = jnp.maximum(old_top, new_top)
    acc = old * jnp.exp2((old_top - best) * SCALE) + new_acc * jnp.exp2((new_top - best) * SCALE)
    state[rows, :] = state_of(best, acc)


def causal(rows, cols, first):
    at = lax.broadcasted_iota(jnp.int32, (rows, cols), 0) + first
    return lax.broadcasted_iota(jnp.int32, (rows, cols), 1) <= at


def short_kernel(at_ref, got_ref, kvm, own_ref, state, qm_ref, ql_ref, kv_buf, one_buf, wide):
    for src in range(HEADS):
        rows = pl.ds(src * BLOCK, BLOCK)
        kv = got_ref[src, :BLOCK]
        kv_buf[rows, :] = kv
        one_buf[rows, :] = with_ones(kv)
    step = 2 * BLOCK
    visible = causal(step, step, 0)
    low = low_lanes(HALF)
    zero = jnp.zeros((HALF, LANES), jnp.bfloat16)
    for i in range(SEG // step):
        parts = []
        for src in (2 * i, 2 * i + 1):
            packed = got_ref[src, BLOCK:PACKED]
            parts.append(jnp.where(low, packed, zero))
            parts.append(jnp.where(low, jnp.concatenate([packed[:, HD:], packed[:, :HD]], axis=1), zero))
        q = jnp.concatenate(parts, axis=0)
        rows = pl.ds(i * step, step)
        wide[rows, :] = q.astype(jnp.float32)
        n = (i + 1) * step
        s = scores_of(q, kv_buf[rows, :])
        s = jnp.where(visible, s, NEGATIVE)
        if i:
            s = jnp.concatenate([scores_of(q, kv_buf[pl.ds(0, i * step), :]), s], axis=1)
        state[rows, :] = state_of(*soft(s, one_buf[pl.ds(0, n), :]))
    o_mid, o_long = own_offsets(at_ref)
    qm_ref[...] = wide[pl.ds(o_mid, N_MID, stride=R_MID), :].astype(jnp.bfloat16)
    ql_ref[...] = wide[pl.ds(o_long, N_LONG, stride=R_LONG), :].astype(jnp.bfloat16)
    for i in range(N_MID // step):
        n = (i + 1) * step
        s = scores_of(qm_ref[pl.ds(i * step, step), :], kvm[:n])
        top, acc = soft(jnp.where(causal(step, n, i * step), s, NEGATIVE), with_ones(kvm[:n]))
        merge(state, pl.ds(o_mid + i * step * R_MID, step, stride=R_MID), top, acc)
    far = own_ref[...]
    s = scores_of(ql_ref[...], far)
    top, acc = soft(jnp.where(causal(N_LONG, N_LONG, 0), s, NEGATIVE), with_ones(far))
    merge(state, pl.ds(o_long, N_LONG, stride=R_LONG), top, acc)


def mid_part(state, qm, o_mid, pos, parts):
    step = 256
    ones = jnp.concatenate([with_ones(ref[...]) for _, ref in parts], axis=0)
    for i in range(N_MID // step):
        q = qm[pl.ds(i * step, step), :]
        pieces = []
        for d, ref in parts:
            before = jnp.bitwise_xor(pos, d) < pos
            pieces.append(scores_of(q, ref[...]) + jnp.where(before, 0.0, NEGATIVE))
        top, new = soft(jnp.concatenate(pieces, axis=1), ones)
        merge(state, pl.ds(o_mid + i * step * R_MID, step, stride=R_MID), top, new)


def long_part(state, ql, o_long, row, its_core, ref):
    every = ref[...].reshape(ROWS // 2 * N_LONG, LANES)
    s = scores_of(ql[...], every)
    before = lax.broadcasted_iota(jnp.int32, s.shape, 1) < ((row + 1 - its_core) // 2) * N_LONG
    top, new = soft(jnp.where(before, s, NEGATIVE), with_ones(every))
    merge(state, pl.ds(o_long, N_LONG, stride=R_LONG), top, new)


def load_rows(src, first, dst, sems):
    count = sems.shape[0]
    part = dst.shape[0] // count
    pairs = [(src.at[pl.ds(first + i * part, part)], dst.at[pl.ds(i * part, part)]) for i in range(count)]
    return fetch(pairs, sems)


def near_kernel(at_ref, state_in, qm, m1, m2, w_hbm, state, w_ref, w_sems):
    loads = load_rows(w_hbm, 0, w_ref, w_sems)
    o_mid, _ = own_offsets(at_ref)
    mid_part(state, qm, o_mid, lax.rem(lax.axis_index("row"), MID_ROWS), ((1, m1), (2, m2)))
    for load in loads:
        load.wait()


def same_kernel(at_ref, state_in, qm, m3, ql, same, state):
    o_mid, o_long = own_offsets(at_ref)
    row = lax.axis_index("row")
    mid_part(state, qm, o_mid, lax.rem(row, MID_ROWS), ((3, m3),))
    long_part(state, ql, o_long, row, lax.rem(row, 2), same)


def last_kernel(at_ref, state_in, ql, other, w_hbm, out_ref, state, w_ref, w_sems):
    loads = load_rows(w_hbm, w_hbm.shape[0] - w_ref.shape[0], w_ref, w_sems)
    _, o_long = own_offsets(at_ref)
    row = lax.axis_index("row")
    long_part(state, ql, o_long, row, 1 - lax.rem(row, 2), other)
    low = low_lanes(HALF)
    for src in range(HEADS):
        done = []
        for half in range(2):
            a = state[pl.ds(src * BLOCK + half * HALF, HALF), :]
            done.append(a / a[:, :1])
        out_ref[src] = jnp.where(low, pltpu.roll(done[0], HD, 1), done[1]).astype(jnp.bfloat16)
    for load in loads:
        load.wait()


def project_kernel(got_ref, w0_ref, w1_ref, out_hbm, combined, tiles, sems):
    count, _, tile = tiles.shape
    for pair in range(HEADS // 2):
        a, b = got_ref[2 * pair], got_ref[2 * pair + 1]
        cols = pl.ds(pair * LANES, LANES)
        combined[:HALF, cols] = jnp.concatenate([a[:, :HD], b[:, :HD]], axis=1)
        combined[HALF:, cols] = jnp.concatenate([a[:, HD:], b[:, HD:]], axis=1)
    cut = w0_ref.shape[0]
    first, second = combined[:, :cut], combined[:, cut:]
    copies = []
    for i in range(count):
        cols = pl.ds(i * tile, tile)
        total = jnp.dot(first, w0_ref[:, cols], preferred_element_type=jnp.float32)
        total += jnp.dot(second, w1_ref[:, cols], preferred_element_type=jnp.float32)
        tiles[i] = total.astype(jnp.bfloat16)
        copies.append(pltpu.make_async_copy(tiles.at[i], out_hbm.at[:, cols], sems.at[i]))
        copies[-1].start()
    for copy in copies:
        copy.wait()


def xor_rows(x, d):
    return lax.ppermute(x, "row", [(i, i ^ d) for i in range(ROWS)])


CORES = [[2 * z + c for z in range(ROWS // 2)] for c in range(2)]
bar = lax.optimization_barrier


def shards(queries, keys, values, mid_offsets, long_offsets, out_weight):
    f32, s32, bf16 = jnp.float32, jnp.int32, jnp.bfloat16
    width = queries.shape[1]
    depth, wide_out = out_weight.shape
    chunks = 4
    sent = call(
        pack_kernel,
        shape(HEADS, PACKED + NOTE, LANES),
        [HB] * 5,
        scratch=[pltpu.SMEM((HEADS,), s32)] * 2
        + [pltpu.VMEM((BLOCK, width), bf16)] * 3
        + [pltpu.VMEM((HEADS, PACKED + NOTE, LANES), bf16), DMA((2,)), DMA((chunks, 3)), DMA((chunks,))],
        moved=1 << 20,
        out_specs=HB,
        limit=VMEM_MOST,
    )(mid_offsets, long_offsets, queries, keys, values)
    got = lax.all_to_all(sent, "col", 0, 0)
    kv_mid, own, at, far = call(
        select_kernel,
        (
            shape(N_MID, LANES),
            shape(N_LONG, LANES),
            shape(NOTE, LANES, dtype=f32),
            shape(ROWS // 2, N_LONG, LANES),
        ),
        [VM],
        scratch=[pltpu.VMEM((SEG, LANES), f32)],
        moved=1 << 20,
    )(got)
    m1 = xor_rows(kv_mid, 1)
    m2 = xor_rows(kv_mid, 2)
    same = lax.all_to_all(far, "row", 0, 0, axis_index_groups=CORES)
    state, q_mid, q_long = call(
        short_kernel,
        (shape(SEG, LANES, dtype=f32), shape(N_MID, LANES), shape(N_LONG, LANES)),
        [VM] * 4,
        scratch=[pltpu.VMEM((SEG, LANES), bf16)] * 2 + [pltpu.VMEM((SEG, LANES), f32)],
        flops=4 * SEG * SEG * LANES,
        moved=3 << 20,
        exps=SEG * SEG // 2,
    )(at, got, kv_mid, own)
    m1, m2, state = bar((m1, m2, state))
    m3 = xor_rows(m2, 1)
    early = depth * 3 // 8
    state, weight0 = call(
        near_kernel,
        (shape(SEG, LANES, dtype=f32), shape(early, wide_out)),
        [VM] * 5 + [HB],
        scratch=[DMA((1,))],
        flops=4 * N_MID * SEG * LANES,
        moved=2 << 20,
        exps=N_MID * SEG,
        aliases={1: 0},
        limit=VMEM_NEAR,
    )(at, state, q_mid, m1, m2, out_weight)
    same, m3, state = bar((same, m3, state))
    other = xor_rows(same, 1)
    state = call(
        same_kernel,
        shape(SEG, LANES, dtype=f32),
        [VM] * 6,
        flops=4 * N_MID * SEG * LANES,
        moved=2 << 20,
        exps=N_MID * SEG,
        aliases={1: 0},
    )(at, state, q_mid, m3, q_long, same)
    tile = 512
    count = wide_out // tile
    back, _, weight = call(
        last_kernel,
        (shape(HEADS, HALF, LANES), shape(SEG, LANES, dtype=f32), shape(depth - early, wide_out)),
        [VM] * 4 + [HB],
        scratch=[DMA((1,))],
        flops=4 * N_LONG * SEG * LANES,
        moved=4 << 20,
        exps=N_LONG * SEG,
        aliases={1: 1},
        limit=VMEM_LAST,
    )(at, state, q_long, other, out_weight)
    return call(
        project_kernel,
        shape(BLOCK, wide_out),
        [VM, VM, VM],
        scratch=[
            pltpu.VMEM((BLOCK, depth), bf16),
            pltpu.VMEM((count, BLOCK, tile), bf16),
            DMA((count,)),
        ],
        flops=2 * BLOCK * depth * wide_out,
        moved=2 * depth * wide_out,
        out_specs=HB,
    )(lax.all_to_all(back, "col", 0, 0), weight0, weight)


def solution(mesh):
    split = P(("row", "col"), None)
    return jax.shard_map(
        shards,
        mesh=mesh,
        in_specs=(split, split, split, P(), P(), P()),
        out_specs=split,
        check_vma=False,
    )
```

```python
import functools

import jax
import jax.numpy as jnp
from jax import lax
from jax.experimental import pallas as pl
from jax.experimental.pallas import tpu as pltpu
from jax.sharding import PartitionSpec as P

R_MID = 4
R_LONG = 16
HEADS = 16
HD = 64
LANES = 128
BLOCK = 128
SEG = 2048
HALF = BLOCK // 2
PACKED = BLOCK + HALF
NOTE = 16
ROWS = 16
MID_ROWS = 4
ZS = ROWS // 2
Z_FIRST = 5
COL_FIRST = 15
N_MID = SEG // R_MID
N_LONG = SEG // R_LONG
NEGATIVE = -1e30
SCALE = 0.125 * 1.4426950408889634
VMEM_LIMIT = 20 * 1024 * 1024
VMEM_LAST = 47 * 1024 * 1024
VMEM_NEAR = 49 * 1024 * 1024
VMEM_MOST = 60 * 1024 * 1024

VM = pl.BlockSpec(memory_space=pltpu.VMEM)
HB = pl.BlockSpec(memory_space=pl.ANY)
DMA = pltpu.SemaphoreType.DMA


def call(
    kernel, out_shape, in_specs, scratch=(), flops=0, moved=0, exps=0, out_specs=None, aliases=None, limit=VMEM_LIMIT
):
    return pl.pallas_call(
        kernel,
        out_shape=out_shape,
        in_specs=in_specs,
        out_specs=jax.tree.map(lambda _: VM, out_shape) if out_specs is None else out_specs,
        scratch_shapes=list(scratch),
        input_output_aliases=aliases or {},
        compiler_params=pltpu.CompilerParams(vmem_limit_bytes=limit),
        cost_estimate=pl.CostEstimate(flops=flops, bytes_accessed=moved, transcendentals=exps),
    )


def shape(*dims, dtype=jnp.bfloat16):
    return jax.ShapeDtypeStruct(dims, dtype)


def low_lanes(rows):
    return lax.broadcasted_iota(jnp.int32, (rows, LANES), 1) < HD


def fetch(pairs, sems):
    copies = [pltpu.make_async_copy(src, dst, sems.at[i]) for i, (src, dst) in enumerate(pairs)]
    for copy in copies:
        copy.start()
    return copies


def slot(col):
    return (col - COL_FIRST) % HEADS


def pack_kernel(
    mid_hbm, long_hbm, q_hbm, k_hbm, v_hbm, out_hbm,
    mid_ref, long_ref, q_ref, k_ref, v_ref, out_ref, at_sems, in_sems, out_sems,
):
    notes = fetch([(mid_hbm, mid_ref), (long_hbm, long_ref)], at_sems)
    chunks = in_sems.shape[0]
    heads = HEADS // chunks
    loads, stores = [], []
    for i in range(chunks):
        cols = pl.ds(i * heads * HD, heads * HD)
        pairs = [(src.at[:, cols], dst.at[:, cols]) for src, dst in ((k_hbm, k_ref), (v_hbm, v_ref), (q_hbm, q_ref))]
        loads.append(fetch(pairs, in_sems.at[i]))
    for copy in notes:
        copy.wait()
    for i in range(chunks):
        for copy in loads[i]:
            copy.wait()
        for head in range(i * heads, i * heads + heads):
            cols = pl.ds(head // 2 * LANES, LANES)
            lanes = slice(head % 2 * HD, head % 2 * HD + HD)
            q = q_ref[:, cols][:, lanes]
            out_ref[slot(head), :BLOCK] = jnp.concatenate([k_ref[:, cols][:, lanes], v_ref[:, cols][:, lanes]], axis=1)
            out_ref[slot(head), BLOCK:PACKED] = jnp.concatenate([q[:HALF], q[HALF:]], axis=1)
            note = jnp.where(low_lanes(NOTE), mid_ref[head].astype(jnp.float32), long_ref[head].astype(jnp.float32))
            out_ref[slot(head), PACKED:] = note.astype(jnp.bfloat16)
        slots = sorted(slot(head) for head in range(i * heads, i * heads + heads))
        runs = [[at for at in slots if at <= slots[0] + heads], [at for at in slots if at > slots[0] + heads]]
        for run in runs:
            if run:
                done = pl.ds(run[0], len(run))
                stores.append(pltpu.make_async_copy(out_ref.at[done], out_hbm.at[done], out_sems.at[len(stores)]))
                stores[-1].start()
    for copy in stores:
        copy.wait()


def select_kernel(got_ref, kvm_ref, own_ref, at_ref, far_ref, wide):
    at_ref[...] = got_ref[0, PACKED:].astype(jnp.float32)
    o_mid, o_long = own_offsets(at_ref)
    for src in range(HEADS):
        wide[pl.ds(src * BLOCK, BLOCK), :] = got_ref[slot(src), :BLOCK].astype(jnp.float32)
    far = wide[pl.ds(o_long, N_LONG, stride=R_LONG), :].astype(jnp.bfloat16)
    own_ref[...] = far
    for z in range(ROWS // 2):
        far_ref[z] = far
    kvm_ref[...] = wide[pl.ds(o_mid, N_MID, stride=R_MID), :].astype(jnp.bfloat16)


def own_offsets(at_ref):
    lane = lax.broadcasted_iota(jnp.int32, at_ref.shape, 1)
    at = at_ref[...].astype(jnp.int32)
    return [jnp.max(jnp.where(lane == where, at, 0)) for where in (0, LANES - 1)]


def scores_of(q, kv):
    return lax.dot_general(q, kv, (((1,), (1,)), ((), ())), preferred_element_type=jnp.float32)


def with_ones(kv):
    return jnp.where(low_lanes(kv.shape[0]), jnp.ones_like(kv), kv)


def soft(s, kv1):
    top = jnp.max(s, axis=1, keepdims=True)
    w = jnp.exp2((s - top) * SCALE).astype(jnp.bfloat16)
    return top, jnp.dot(w, kv1, preferred_element_type=jnp.float32)


def state_of(top, acc):
    lane = lax.broadcasted_iota(jnp.int32, acc.shape, 1)
    return jnp.where((lane >= HD // 2) & (lane < HD), top, acc)


def merge(state, rows, new_top, new_acc):
    old = state[rows, :]
    old_top = old[:, HD // 2 : HD // 2 + 1]
    best = jnp.maximum(old_top, new_top)
    acc = old * jnp.exp2((old_top - best) * SCALE) + new_acc * jnp.exp2((new_top - best) * SCALE)
    state[rows, :] = state_of(best, acc)


def causal(rows, cols, first):
    at = lax.broadcasted_iota(jnp.int32, (rows, cols), 0) + first
    return lax.broadcasted_iota(jnp.int32, (rows, cols), 1) <= at


def short_kernel(at_ref, got_ref, kvm, own_ref, state, qm_ref, ql_ref, kv_buf, one_buf, wide):
    for src in range(HEADS):
        rows = pl.ds(src * BLOCK, BLOCK)
        kv = got_ref[slot(src), :BLOCK]
        kv_buf[rows, :] = kv
        one_buf[rows, :] = with_ones(kv)
    step = 2 * BLOCK
    visible = causal(step, step, 0)
    low = low_lanes(HALF)
    zero = jnp.zeros((HALF, LANES), jnp.bfloat16)
    for i in range(SEG // step):
        parts = []
        for src in (2 * i, 2 * i + 1):
            packed = got_ref[slot(src), BLOCK:PACKED]
            parts.append(jnp.where(low, packed, zero))
            parts.append(jnp.where(low, jnp.concatenate([packed[:, HD:], packed[:, :HD]], axis=1), zero))
        q = jnp.concatenate(parts, axis=0)
        rows = pl.ds(i * step, step)
        wide[rows, :] = q.astype(jnp.float32)
        n = (i + 1) * step
        s = scores_of(q, kv_buf[rows, :])
        s = jnp.where(visible, s, NEGATIVE)
        if i:
            s = jnp.concatenate([scores_of(q, kv_buf[pl.ds(0, i * step), :]), s], axis=1)
        state[rows, :] = state_of(*soft(s, one_buf[pl.ds(0, n), :]))
    o_mid, o_long = own_offsets(at_ref)
    qm_ref[...] = wide[pl.ds(o_mid, N_MID, stride=R_MID), :].astype(jnp.bfloat16)
    ql_ref[...] = wide[pl.ds(o_long, N_LONG, stride=R_LONG), :].astype(jnp.bfloat16)
    for i in range(N_MID // step):
        n = (i + 1) * step
        s = scores_of(qm_ref[pl.ds(i * step, step), :], kvm[:n])
        top, acc = soft(jnp.where(causal(step, n, i * step), s, NEGATIVE), with_ones(kvm[:n]))
        merge(state, pl.ds(o_mid + i * step * R_MID, step, stride=R_MID), top, acc)
    far = own_ref[...]
    s = scores_of(ql_ref[...], far)
    top, acc = soft(jnp.where(causal(N_LONG, N_LONG, 0), s, NEGATIVE), with_ones(far))
    merge(state, pl.ds(o_long, N_LONG, stride=R_LONG), top, acc)


def mid_part(state, qm, o_mid, pos, parts):
    step = 256
    ones = jnp.concatenate([with_ones(ref[...]) for _, ref in parts], axis=0)
    for i in range(N_MID // step):
        q = qm[pl.ds(i * step, step), :]
        pieces = []
        for d, ref in parts:
            before = jnp.bitwise_xor(pos, d) < pos
            pieces.append(scores_of(q, ref[...]) + jnp.where(before, 0.0, NEGATIVE))
        top, new = soft(jnp.concatenate(pieces, axis=1), ones)
        merge(state, pl.ds(o_mid + i * step * R_MID, step, stride=R_MID), top, new)


def long_part(state, ql, o_long, row, its_core, ref):
    every = ref[...].reshape(ZS * N_LONG, LANES)
    s = scores_of(ql[...], every)
    z = (lax.broadcasted_iota(jnp.int32, s.shape, 1) // N_LONG + Z_FIRST) % ZS
    before = 2 * z + its_core < row
    top, new = soft(jnp.where(before, s, NEGATIVE), with_ones(every))
    merge(state, pl.ds(o_long, N_LONG, stride=R_LONG), top, new)


def load_rows(src, first, dst, sems):
    count = sems.shape[0]
    part = dst.shape[0] // count
    pairs = [(src.at[pl.ds(first + i * part, part)], dst.at[pl.ds(i * part, part)]) for i in range(count)]
    return fetch(pairs, sems)


def near_kernel(at_ref, state_in, qm, m1, m2, w_hbm, state, w_ref, w_sems):
    loads = load_rows(w_hbm, 0, w_ref, w_sems)
    o_mid, _ = own_offsets(at_ref)
    mid_part(state, qm, o_mid, lax.rem(lax.axis_index("row"), MID_ROWS), ((1, m1), (2, m2)))
    for load in loads:
        load.wait()


def same_kernel(at_ref, state_in, qm, m3, ql, same, state):
    o_mid, o_long = own_offsets(at_ref)
    row = lax.axis_index("row")
    mid_part(state, qm, o_mid, lax.rem(row, MID_ROWS), ((3, m3),))
    long_part(state, ql, o_long, row, lax.rem(row, 2), same)


def last_kernel(at_ref, state_in, ql, other, w_hbm, out_ref, state, w_ref, w_sems):
    loads = load_rows(w_hbm, w_hbm.shape[0] - w_ref.shape[0], w_ref, w_sems)
    _, o_long = own_offsets(at_ref)
    row = lax.axis_index("row")
    long_part(state, ql, o_long, row, 1 - lax.rem(row, 2), other)
    low = low_lanes(HALF)
    for src in range(HEADS):
        done = []
        for half in range(2):
            a = state[pl.ds(src * BLOCK + half * HALF, HALF), :]
            done.append(a / a[:, :1])
        out_ref[src] = jnp.where(low, pltpu.roll(done[0], HD, 1), done[1]).astype(jnp.bfloat16)
    for load in loads:
        load.wait()


def project_kernel(got_ref, w0_ref, w1_ref, out_hbm, combined, tiles, sems):
    count, _, tile = tiles.shape
    for pair in range(HEADS // 2):
        a, b = got_ref[2 * pair], got_ref[2 * pair + 1]
        cols = pl.ds(pair * LANES, LANES)
        combined[:HALF, cols] = jnp.concatenate([a[:, :HD], b[:, :HD]], axis=1)
        combined[HALF:, cols] = jnp.concatenate([a[:, HD:], b[:, HD:]], axis=1)
    cut = w0_ref.shape[0]
    first, second = combined[:, :cut], combined[:, cut:]
    copies = []
    for i in range(count):
        cols = pl.ds(i * tile, tile)
        total = jnp.dot(first, w0_ref[:, cols], preferred_element_type=jnp.float32)
        total += jnp.dot(second, w1_ref[:, cols], preferred_element_type=jnp.float32)
        tiles[i] = total.astype(jnp.bfloat16)
        copies.append(pltpu.make_async_copy(tiles.at[i], out_hbm.at[:, cols], sems.at[i]))
        copies[-1].start()
    for copy in copies:
        copy.wait()


def xor_rows(x, d):
    return lax.ppermute(x, "row", [(i, i ^ d) for i in range(ROWS)])


CORES = [[2 * ((p + Z_FIRST) % ZS) + c for p in range(ZS)] for c in range(2)]
COLS = [[(p + COL_FIRST) % HEADS for p in range(HEADS)]]
bar = lax.optimization_barrier


def shards(queries, keys, values, mid_offsets, long_offsets, out_weight):
    f32, s32, bf16 = jnp.float32, jnp.int32, jnp.bfloat16
    width = queries.shape[1]
    depth, wide_out = out_weight.shape
    chunks = 4
    sent = call(
        pack_kernel,
        shape(HEADS, PACKED + NOTE, LANES),
        [HB] * 5,
        scratch=[pltpu.SMEM((HEADS,), s32)] * 2
        + [pltpu.VMEM((BLOCK, width), bf16)] * 3
        + [pltpu.VMEM((HEADS, PACKED + NOTE, LANES), bf16), DMA((2,)), DMA((chunks, 3)), DMA((chunks + 1,))],
        moved=1 << 20,
        out_specs=HB,
        limit=VMEM_MOST,
    )(mid_offsets, long_offsets, queries, keys, values)
    got = lax.all_to_all(sent, "col", 0, 0, axis_index_groups=COLS)
    kv_mid, own, at, far = call(
        select_kernel,
        (
            shape(N_MID, LANES),
            shape(N_LONG, LANES),
            shape(NOTE, LANES, dtype=f32),
            shape(ROWS // 2, N_LONG, LANES),
        ),
        [VM],
        scratch=[pltpu.VMEM((SEG, LANES), f32)],
        moved=1 << 20,
    )(got)
    m1 = xor_rows(kv_mid, 1)
    m2 = xor_rows(kv_mid, 2)
    same = lax.all_to_all(far, "row", 0, 0, axis_index_groups=CORES)
    state, q_mid, q_long = call(
        short_kernel,
        (shape(SEG, LANES, dtype=f32), shape(N_MID, LANES), shape(N_LONG, LANES)),
        [VM] * 4,
        scratch=[pltpu.VMEM((SEG, LANES), bf16)] * 2 + [pltpu.VMEM((SEG, LANES), f32)],
        flops=4 * SEG * SEG * LANES,
        moved=3 << 20,
        exps=SEG * SEG // 2,
    )(at, got, kv_mid, own)
    m1, m2, state = bar((m1, m2, state))
    m3 = xor_rows(m2, 1)
    early = depth * 3 // 8
    state, weight0 = call(
        near_kernel,
        (shape(SEG, LANES, dtype=f32), shape(early, wide_out)),
        [VM] * 5 + [HB],
        scratch=[DMA((1,))],
        flops=4 * N_MID * SEG * LANES,
        moved=2 << 20,
        exps=N_MID * SEG,
        aliases={1: 0},
        limit=VMEM_NEAR,
    )(at, state, q_mid, m1, m2, out_weight)
    same, m3, state = bar((same, m3, state))
    other = xor_rows(same, 1)
    state = call(
        same_kernel,
        shape(SEG, LANES, dtype=f32),
        [VM] * 6,
        flops=4 * N_MID * SEG * LANES,
        moved=2 << 20,
        exps=N_MID * SEG,
        aliases={1: 0},
    )(at, state, q_mid, m3, q_long, same)
    tile = 512
    count = wide_out // tile
    back, _, weight = call(
        last_kernel,
        (shape(HEADS, HALF, LANES), shape(SEG, LANES, dtype=f32), shape(depth - early, wide_out)),
        [VM] * 4 + [HB],
        scratch=[DMA((1,))],
        flops=4 * N_LONG * SEG * LANES,
        moved=4 << 20,
        exps=N_LONG * SEG,
        aliases={1: 1},
        limit=VMEM_LAST,
    )(at, state, q_long, other, out_weight)
    return call(
        project_kernel,
        shape(BLOCK, wide_out),
        [VM, VM, VM],
        scratch=[
            pltpu.VMEM((BLOCK, depth), bf16),
            pltpu.VMEM((count, BLOCK, tile), bf16),
            DMA((count,)),
        ],
        flops=2 * BLOCK * depth * wide_out,
        moved=2 * depth * wide_out,
        out_specs=HB,
    )(lax.all_to_all(back, "col", 0, 0), weight0, weight)


def solution(mesh):
    split = P(("row", "col"), None)
    return jax.shard_map(
        shards,
        mesh=mesh,
        in_specs=(split, split, split, P(), P(), P()),
        out_specs=split,
        check_vma=False,
    )
```

```python
import functools

import jax
import jax.numpy as jnp
from jax import lax
from jax.experimental import pallas as pl
from jax.experimental.pallas import tpu as pltpu
from jax.sharding import PartitionSpec as P

R_MID = 4
R_LONG = 16
HEADS = 16
HD = 64
LANES = 128
BLOCK = 128
SEG = 2048
HALF = BLOCK // 2
PACKED = BLOCK + HALF
NOTE = 16
ROWS = 16
MID_ROWS = 4
ZS = ROWS // 2
Z_FIRST = 5
COL_FIRST = 15
N_MID = SEG // R_MID
N_LONG = SEG // R_LONG
NEGATIVE = -1e30
SCALE = 0.125 * 1.4426950408889634
VMEM_LIMIT = 20 * 1024 * 1024
VMEM_LAST = 47 * 1024 * 1024
VMEM_NEAR = 49 * 1024 * 1024
VMEM_MOST = 60 * 1024 * 1024

VM = pl.BlockSpec(memory_space=pltpu.VMEM)
HB = pl.BlockSpec(memory_space=pl.ANY)
DMA = pltpu.SemaphoreType.DMA


def call(
    kernel, out_shape, in_specs, scratch=(), flops=0, moved=0, exps=0, out_specs=None, aliases=None, limit=VMEM_LIMIT
):
    return pl.pallas_call(
        kernel,
        out_shape=out_shape,
        in_specs=in_specs,
        out_specs=jax.tree.map(lambda _: VM, out_shape) if out_specs is None else out_specs,
        scratch_shapes=list(scratch),
        input_output_aliases=aliases or {},
        compiler_params=pltpu.CompilerParams(vmem_limit_bytes=limit),
        cost_estimate=pl.CostEstimate(flops=flops, bytes_accessed=moved, transcendentals=exps),
    )


def shape(*dims, dtype=jnp.bfloat16):
    return jax.ShapeDtypeStruct(dims, dtype)


def low_lanes(rows):
    return lax.broadcasted_iota(jnp.int32, (rows, LANES), 1) < HD


def fetch(pairs, sems):
    copies = [pltpu.make_async_copy(src, dst, sems.at[i]) for i, (src, dst) in enumerate(pairs)]
    for copy in copies:
        copy.start()
    return copies


def slot(col):
    return (col - COL_FIRST) % HEADS


def pack_kernel(
    mid_hbm, long_hbm, q_hbm, k_hbm, v_hbm, out_hbm,
    mid_ref, long_ref, q_ref, k_ref, v_ref, out_ref, at_sems, in_sems, out_sems,
):
    notes = fetch([(mid_hbm, mid_ref), (long_hbm, long_ref)], at_sems)
    chunks = in_sems.shape[0]
    heads = HEADS // chunks
    loads, stores = [], []
    for i in range(chunks):
        cols = pl.ds(i * heads * HD, heads * HD)
        pairs = [(src.at[:, cols], dst.at[:, cols]) for src, dst in ((k_hbm, k_ref), (v_hbm, v_ref), (q_hbm, q_ref))]
        loads.append(fetch(pairs, in_sems.at[i]))
    for copy in notes:
        copy.wait()
    for i in range(chunks):
        for copy in loads[i]:
            copy.wait()
        for head in range(i * heads, i * heads + heads):
            cols = pl.ds(head // 2 * LANES, LANES)
            lanes = slice(head % 2 * HD, head % 2 * HD + HD)
            q = q_ref[:, cols][:, lanes]
            out_ref[slot(head), :BLOCK] = jnp.concatenate([k_ref[:, cols][:, lanes], v_ref[:, cols][:, lanes]], axis=1)
            out_ref[slot(head), BLOCK:PACKED] = jnp.concatenate([q[:HALF], q[HALF:]], axis=1)
            note = jnp.where(low_lanes(NOTE), mid_ref[head].astype(jnp.float32), long_ref[head].astype(jnp.float32))
            out_ref[slot(head), PACKED:] = note.astype(jnp.bfloat16)
        slots = sorted(slot(head) for head in range(i * heads, i * heads + heads))
        runs = [[at for at in slots if at <= slots[0] + heads], [at for at in slots if at > slots[0] + heads]]
        for run in runs:
            if run:
                done = pl.ds(run[0], len(run))
                stores.append(pltpu.make_async_copy(out_ref.at[done], out_hbm.at[done], out_sems.at[len(stores)]))
                stores[-1].start()
    for copy in stores:
        copy.wait()


def select_kernel(got_ref, kvm_ref, own_ref, at_ref, far_ref, wide):
    at_ref[...] = got_ref[0, PACKED:].astype(jnp.float32)
    o_mid, o_long = own_offsets(at_ref)
    for src in range(HEADS):
        wide[pl.ds(src * BLOCK, BLOCK), :] = got_ref[slot(src), :BLOCK].astype(jnp.float32)
    far = wide[pl.ds(o_long, N_LONG, stride=R_LONG), :].astype(jnp.bfloat16)
    own_ref[...] = far
    for z in range(ROWS // 2):
        far_ref[z] = far
    kvm_ref[...] = wide[pl.ds(o_mid, N_MID, stride=R_MID), :].astype(jnp.bfloat16)


def own_offsets(at_ref):
    lane = lax.broadcasted_iota(jnp.int32, at_ref.shape, 1)
    at = at_ref[...].astype(jnp.int32)
    return [jnp.max(jnp.where(lane == where, at, 0)) for where in (0, LANES - 1)]


def scores_of(q, kv):
    return lax.dot_general(q, kv, (((1,), (1,)), ((), ())), preferred_element_type=jnp.float32)


def with_ones(kv):
    return jnp.where(low_lanes(kv.shape[0]), jnp.ones_like(kv), kv)


def soft(s, kv1):
    top = jnp.max(s, axis=1, keepdims=True)
    w = jnp.exp2((s - top) * SCALE).astype(jnp.bfloat16)
    return top, jnp.dot(w, kv1, preferred_element_type=jnp.float32)


def state_of(top, acc):
    lane = lax.broadcasted_iota(jnp.int32, acc.shape, 1)
    return jnp.where((lane >= HD // 2) & (lane < HD), top, acc)


def merge(state, rows, new_top, new_acc):
    old = state[rows, :]
    old_top = old[:, HD // 2 : HD // 2 + 1]
    best = jnp.maximum(old_top, new_top)
    acc = old * jnp.exp2((old_top - best) * SCALE) + new_acc * jnp.exp2((new_top - best) * SCALE)
    state[rows, :] = state_of(best, acc)


def causal(rows, cols, first):
    at = lax.broadcasted_iota(jnp.int32, (rows, cols), 0) + first
    return lax.broadcasted_iota(jnp.int32, (rows, cols), 1) <= at


def short_kernel(at_ref, got_ref, kvm, own_ref, state, qm_ref, ql_ref, kv_buf, one_buf, wide):
    for src in range(HEADS):
        rows = pl.ds(src * BLOCK, BLOCK)
        kv = got_ref[slot(src), :BLOCK]
        kv_buf[rows, :] = kv
        one_buf[rows, :] = with_ones(kv)
    step = 2 * BLOCK
    visible = causal(step, step, 0)
    low = low_lanes(HALF)
    zero = jnp.zeros((HALF, LANES), jnp.bfloat16)
    for i in range(SEG // step):
        parts = []
        for src in (2 * i, 2 * i + 1):
            packed = got_ref[slot(src), BLOCK:PACKED]
            parts.append(jnp.where(low, packed, zero))
            parts.append(jnp.where(low, jnp.concatenate([packed[:, HD:], packed[:, :HD]], axis=1), zero))
        q = jnp.concatenate(parts, axis=0)
        rows = pl.ds(i * step, step)
        wide[rows, :] = q.astype(jnp.float32)
        n = (i + 1) * step
        s = scores_of(q, kv_buf[rows, :])
        s = jnp.where(visible, s, NEGATIVE)
        if i:
            s = jnp.concatenate([scores_of(q, kv_buf[pl.ds(0, i * step), :]), s], axis=1)
        state[rows, :] = state_of(*soft(s, one_buf[pl.ds(0, n), :]))
    o_mid, o_long = own_offsets(at_ref)
    qm_ref[...] = wide[pl.ds(o_mid, N_MID, stride=R_MID), :].astype(jnp.bfloat16)
    ql_ref[...] = wide[pl.ds(o_long, N_LONG, stride=R_LONG), :].astype(jnp.bfloat16)
    for i in range(N_MID // step):
        n = (i + 1) * step
        s = scores_of(qm_ref[pl.ds(i * step, step), :], kvm[:n])
        top, acc = soft(jnp.where(causal(step, n, i * step), s, NEGATIVE), with_ones(kvm[:n]))
        merge(state, pl.ds(o_mid + i * step * R_MID, step, stride=R_MID), top, acc)
    far = own_ref[...]
    s = scores_of(ql_ref[...], far)
    top, acc = soft(jnp.where(causal(N_LONG, N_LONG, 0), s, NEGATIVE), with_ones(far))
    merge(state, pl.ds(o_long, N_LONG, stride=R_LONG), top, acc)


def mid_part(state, qm, o_mid, pos, parts):
    step = 256
    ones = jnp.concatenate([with_ones(ref[...]) for _, ref in parts], axis=0)
    for i in range(N_MID // step):
        q = qm[pl.ds(i * step, step), :]
        pieces = []
        for d, ref in parts:
            before = jnp.bitwise_xor(pos, d) < pos
            pieces.append(scores_of(q, ref[...]) + jnp.where(before, 0.0, NEGATIVE))
        top, new = soft(jnp.concatenate(pieces, axis=1), ones)
        merge(state, pl.ds(o_mid + i * step * R_MID, step, stride=R_MID), top, new)


def long_part(state, ql, o_long, row, its_core, ref):
    every = ref[...].reshape(ZS * N_LONG, LANES)
    s = scores_of(ql[...], every)
    z = (lax.broadcasted_iota(jnp.int32, s.shape, 1) // N_LONG + Z_FIRST) % ZS
    before = 2 * z + its_core < row
    top, new = soft(jnp.where(before, s, NEGATIVE), with_ones(every))
    merge(state, pl.ds(o_long, N_LONG, stride=R_LONG), top, new)


def load_rows(src, first, dst, sems):
    count = sems.shape[0]
    part = dst.shape[0] // count
    pairs = [(src.at[pl.ds(first + i * part, part)], dst.at[pl.ds(i * part, part)]) for i in range(count)]
    return fetch(pairs, sems)


def near_kernel(at_ref, state_in, qm, m1, m2, w_hbm, state, w_ref, w_sems):
    loads = load_rows(w_hbm, 0, w_ref, w_sems)
    o_mid, _ = own_offsets(at_ref)
    mid_part(state, qm, o_mid, lax.rem(lax.axis_index("row"), MID_ROWS), ((1, m1), (2, m2)))
    for load in loads:
        load.wait()


def same_kernel(at_ref, state_in, qm, m3, ql, same, state):
    o_mid, o_long = own_offsets(at_ref)
    row = lax.axis_index("row")
    mid_part(state, qm, o_mid, lax.rem(row, MID_ROWS), ((3, m3),))
    long_part(state, ql, o_long, row, lax.rem(row, 2), same)


def last_kernel(at_ref, state_in, ql, other, w_hbm, out_ref, state, w_ref, w_sems):
    loads = load_rows(w_hbm, w_hbm.shape[0] - w_ref.shape[0], w_ref, w_sems)
    _, o_long = own_offsets(at_ref)
    row = lax.axis_index("row")
    long_part(state, ql, o_long, row, 1 - lax.rem(row, 2), other)
    low = low_lanes(HALF)
    for src in range(HEADS):
        done = []
        for half in range(2):
            a = state[pl.ds(src * BLOCK + half * HALF, HALF), :]
            done.append(a / a[:, :1])
        out_ref[slot(src)] = jnp.where(low, pltpu.roll(done[0], HD, 1), done[1]).astype(jnp.bfloat16)
    for load in loads:
        load.wait()


def project_kernel(got_ref, w0_ref, w1_ref, out_hbm, combined, tiles, sems):
    count, _, tile = tiles.shape
    for pair in range(HEADS // 2):
        a, b = got_ref[slot(2 * pair)], got_ref[slot(2 * pair + 1)]
        cols = pl.ds(pair * LANES, LANES)
        combined[:HALF, cols] = jnp.concatenate([a[:, :HD], b[:, :HD]], axis=1)
        combined[HALF:, cols] = jnp.concatenate([a[:, HD:], b[:, HD:]], axis=1)
    cut = w0_ref.shape[0]
    first, second = combined[:, :cut], combined[:, cut:]
    copies = []
    for i in range(count):
        cols = pl.ds(i * tile, tile)
        total = jnp.dot(first, w0_ref[:, cols], preferred_element_type=jnp.float32)
        total += jnp.dot(second, w1_ref[:, cols], preferred_element_type=jnp.float32)
        tiles[i] = total.astype(jnp.bfloat16)
        copies.append(pltpu.make_async_copy(tiles.at[i], out_hbm.at[:, cols], sems.at[i]))
        copies[-1].start()
    for copy in copies:
        copy.wait()


def xor_rows(x, d):
    return lax.ppermute(x, "row", [(i, i ^ d) for i in range(ROWS)])


CORES = [[2 * ((p + Z_FIRST) % ZS) + c for p in range(ZS)] for c in range(2)]
COLS = [[(p + COL_FIRST) % HEADS for p in range(HEADS)]]
bar = lax.optimization_barrier


def shards(queries, keys, values, mid_offsets, long_offsets, out_weight):
    f32, s32, bf16 = jnp.float32, jnp.int32, jnp.bfloat16
    width = queries.shape[1]
    depth, wide_out = out_weight.shape
    chunks = 4
    sent = call(
        pack_kernel,
        shape(HEADS, PACKED + NOTE, LANES),
        [HB] * 5,
        scratch=[pltpu.SMEM((HEADS,), s32)] * 2
        + [pltpu.VMEM((BLOCK, width), bf16)] * 3
        + [pltpu.VMEM((HEADS, PACKED + NOTE, LANES), bf16), DMA((2,)), DMA((chunks, 3)), DMA((chunks + 1,))],
        moved=1 << 20,
        out_specs=HB,
        limit=VMEM_MOST,
    )(mid_offsets, long_offsets, queries, keys, values)
    got = lax.all_to_all(sent, "col", 0, 0, axis_index_groups=COLS)
    kv_mid, own, at, far = call(
        select_kernel,
        (
            shape(N_MID, LANES),
            shape(N_LONG, LANES),
            shape(NOTE, LANES, dtype=f32),
            shape(ROWS // 2, N_LONG, LANES),
        ),
        [VM],
        scratch=[pltpu.VMEM((SEG, LANES), f32)],
        moved=1 << 20,
    )(got)
    m1 = xor_rows(kv_mid, 1)
    m2 = xor_rows(kv_mid, 2)
    same = lax.all_to_all(far, "row", 0, 0, axis_index_groups=CORES)
    state, q_mid, q_long = call(
        short_kernel,
        (shape(SEG, LANES, dtype=f32), shape(N_MID, LANES), shape(N_LONG, LANES)),
        [VM] * 4,
        scratch=[pltpu.VMEM((SEG, LANES), bf16)] * 2 + [pltpu.VMEM((SEG, LANES), f32)],
        flops=4 * SEG * SEG * LANES,
        moved=3 << 20,
        exps=SEG * SEG // 2,
    )(at, got, kv_mid, own)
    m1, m2, state = bar((m1, m2, state))
    m3 = xor_rows(m2, 1)
    early = depth * 3 // 8
    state, weight0 = call(
        near_kernel,
        (shape(SEG, LANES, dtype=f32), shape(early, wide_out)),
        [VM] * 5 + [HB],
        scratch=[DMA((1,))],
        flops=4 * N_MID * SEG * LANES,
        moved=2 << 20,
        exps=N_MID * SEG,
        aliases={1: 0},
        limit=VMEM_NEAR,
    )(at, state, q_mid, m1, m2, out_weight)
    same, m3, state = bar((same, m3, state))
    other = xor_rows(same, 1)
    state = call(
        same_kernel,
        shape(SEG, LANES, dtype=f32),
        [VM] * 6,
        flops=4 * N_MID * SEG * LANES,
        moved=2 << 20,
        exps=N_MID * SEG,
        aliases={1: 0},
    )(at, state, q_mid, m3, q_long, same)
    tile = 512
    count = wide_out // tile
    back, _, weight = call(
        last_kernel,
        (shape(HEADS, HALF, LANES), shape(SEG, LANES, dtype=f32), shape(depth - early, wide_out)),
        [VM] * 4 + [HB],
        scratch=[DMA((1,))],
        flops=4 * N_LONG * SEG * LANES,
        moved=4 << 20,
        exps=N_LONG * SEG,
        aliases={1: 1},
        limit=VMEM_LAST,
    )(at, state, q_long, other, out_weight)
    return call(
        project_kernel,
        shape(BLOCK, wide_out),
        [VM, VM, VM],
        scratch=[
            pltpu.VMEM((BLOCK, depth), bf16),
            pltpu.VMEM((count, BLOCK, tile), bf16),
            DMA((count,)),
        ],
        flops=2 * BLOCK * depth * wide_out,
        moved=2 * depth * wide_out,
        out_specs=HB,
    )(lax.all_to_all(back, "col", 0, 0, axis_index_groups=COLS), weight0, weight)


def solution(mesh):
    split = P(("row", "col"), None)
    return jax.shard_map(
        shards,
        mesh=mesh,
        in_specs=(split, split, split, P(), P(), P()),
        out_specs=split,
        check_vma=False,
    )
```

```python
import functools

import jax
import jax.numpy as jnp
from jax import lax
from jax.experimental import pallas as pl
from jax.experimental.pallas import tpu as pltpu
from jax.sharding import PartitionSpec as P

R_MID = 4
R_LONG = 16
HEADS = 16
HD = 64
LANES = 128
BLOCK = 128
SEG = 2048
HALF = BLOCK // 2
PACKED = BLOCK + HALF
NOTE = 16
ROWS = 16
MID_ROWS = 4
ZS = ROWS // 2
Z_FIRST = 5
COL_FIRST = 15
N_MID = SEG // R_MID
N_LONG = SEG // R_LONG
NEGATIVE = -1e30
SCALE = 0.125 * 1.4426950408889634
VMEM_LIMIT = 20 * 1024 * 1024
VMEM_LAST = 47 * 1024 * 1024
VMEM_NEAR = 49 * 1024 * 1024
VMEM_MOST = 60 * 1024 * 1024

VM = pl.BlockSpec(memory_space=pltpu.VMEM)
HB = pl.BlockSpec(memory_space=pl.ANY)
DMA = pltpu.SemaphoreType.DMA


def call(
    kernel, out_shape, in_specs, scratch=(), flops=0, moved=0, exps=0, out_specs=None, aliases=None, limit=VMEM_LIMIT
):
    return pl.pallas_call(
        kernel,
        out_shape=out_shape,
        in_specs=in_specs,
        out_specs=jax.tree.map(lambda _: VM, out_shape) if out_specs is None else out_specs,
        scratch_shapes=list(scratch),
        input_output_aliases=aliases or {},
        compiler_params=pltpu.CompilerParams(vmem_limit_bytes=limit),
        cost_estimate=pl.CostEstimate(flops=flops, bytes_accessed=moved, transcendentals=exps),
    )


def shape(*dims, dtype=jnp.bfloat16):
    return jax.ShapeDtypeStruct(dims, dtype)


def low_lanes(rows):
    return lax.broadcasted_iota(jnp.int32, (rows, LANES), 1) < HD


def fetch(pairs, sems):
    copies = [pltpu.make_async_copy(src, dst, sems.at[i]) for i, (src, dst) in enumerate(pairs)]
    for copy in copies:
        copy.start()
    return copies


def slot(col):
    return (col - COL_FIRST) % HEADS


def pack_kernel(
    mid_hbm, long_hbm, q_hbm, k_hbm, v_hbm, out_hbm,
    mid_ref, long_ref, q_ref, k_ref, v_ref, out_ref, at_sems, in_sems, out_sems,
):
    notes = fetch([(mid_hbm, mid_ref), (long_hbm, long_ref)], at_sems)
    chunks = in_sems.shape[0]
    heads = HEADS // chunks
    loads, stores = [], []
    for i in range(chunks):
        cols = pl.ds(i * heads * HD, heads * HD)
        pairs = [(src.at[:, cols], dst.at[:, cols]) for src, dst in ((k_hbm, k_ref), (v_hbm, v_ref), (q_hbm, q_ref))]
        loads.append(fetch(pairs, in_sems.at[i]))
    for copy in notes:
        copy.wait()
    for i in range(chunks):
        for copy in loads[i]:
            copy.wait()
        for head in range(i * heads, i * heads + heads):
            cols = pl.ds(head // 2 * LANES, LANES)
            lanes = slice(head % 2 * HD, head % 2 * HD + HD)
            q = q_ref[:, cols][:, lanes]
            out_ref[slot(head), :BLOCK] = jnp.concatenate([k_ref[:, cols][:, lanes], v_ref[:, cols][:, lanes]], axis=1)
            out_ref[slot(head), BLOCK:PACKED] = jnp.concatenate([q[:HALF], q[HALF:]], axis=1)
            note = jnp.where(low_lanes(NOTE), mid_ref[head].astype(jnp.float32), long_ref[head].astype(jnp.float32))
            out_ref[slot(head), PACKED:] = note.astype(jnp.bfloat16)
        slots = sorted(slot(head) for head in range(i * heads, i * heads + heads))
        runs = [[at for at in slots if at <= slots[0] + heads], [at for at in slots if at > slots[0] + heads]]
        for run in runs:
            if run:
                done = pl.ds(run[0], len(run))
                stores.append(pltpu.make_async_copy(out_ref.at[done], out_hbm.at[done], out_sems.at[len(stores)]))
                stores[-1].start()
    for copy in stores:
        copy.wait()


def select_kernel(got_ref, kvm_ref, own_ref, at_ref, far_ref, wide):
    at_ref[...] = got_ref[0, PACKED:].astype(jnp.float32)
    o_mid, o_long = own_offsets(at_ref)
    for src in range(HEADS):
        wide[pl.ds(src * BLOCK, BLOCK), :] = got_ref[slot(src), :BLOCK].astype(jnp.float32)
    far = wide[pl.ds(o_long, N_LONG, stride=R_LONG), :].astype(jnp.bfloat16)
    own_ref[...] = far
    for z in range(ROWS // 2):
        far_ref[z] = far
    kvm_ref[...] = wide[pl.ds(o_mid, N_MID, stride=R_MID), :].astype(jnp.bfloat16)


def own_offsets(at_ref):
    lane = lax.broadcasted_iota(jnp.int32, at_ref.shape, 1)
    at = at_ref[...].astype(jnp.int32)
    return [jnp.max(jnp.where(lane == where, at, 0)) for where in (0, LANES - 1)]


def scores_of(q, kv):
    return lax.dot_general(q, kv, (((1,), (1,)), ((), ())), preferred_element_type=jnp.float32)


def with_ones(kv):
    return jnp.where(low_lanes(kv.shape[0]), jnp.ones_like(kv), kv)


def soft(s, kv1):
    top = jnp.max(s, axis=1, keepdims=True)
    w = jnp.exp2((s - top) * SCALE).astype(jnp.bfloat16)
    return top, jnp.dot(w, kv1, preferred_element_type=jnp.float32)


def state_of(top, acc):
    lane = lax.broadcasted_iota(jnp.int32, acc.shape, 1)
    return jnp.where((lane >= HD // 2) & (lane < HD), top, acc)


def merge(state, rows, new_top, new_acc):
    old = state[rows, :]
    old_top = old[:, HD // 2 : HD // 2 + 1]
    best = jnp.maximum(old_top, new_top)
    acc = old * jnp.exp2((old_top - best) * SCALE) + new_acc * jnp.exp2((new_top - best) * SCALE)
    state[rows, :] = state_of(best, acc)


def causal(rows, cols, first):
    at = lax.broadcasted_iota(jnp.int32, (rows, cols), 0) + first
    return lax.broadcasted_iota(jnp.int32, (rows, cols), 1) <= at


def short_kernel(at_ref, got_ref, kvm, own_ref, state, qm_ref, ql_ref, kv_buf, one_buf, wide):
    for src in range(HEADS):
        rows = pl.ds(src * BLOCK, BLOCK)
        kv = got_ref[slot(src), :BLOCK]
        kv_buf[rows, :] = kv
        one_buf[rows, :] = with_ones(kv)
    step = 2 * BLOCK
    visible = causal(step, step, 0)
    low = low_lanes(HALF)
    zero = jnp.zeros((HALF, LANES), jnp.bfloat16)
    for i in range(SEG // step):
        parts = []
        for src in (2 * i, 2 * i + 1):
            packed = got_ref[slot(src), BLOCK:PACKED]
            parts.append(jnp.where(low, packed, zero))
            parts.append(jnp.where(low, jnp.concatenate([packed[:, HD:], packed[:, :HD]], axis=1), zero))
        q = jnp.concatenate(parts, axis=0)
        rows = pl.ds(i * step, step)
        wide[rows, :] = q.astype(jnp.float32)
        n = (i + 1) * step
        s = scores_of(q, kv_buf[rows, :])
        s = jnp.where(visible, s, NEGATIVE)
        if i:
            s = jnp.concatenate([scores_of(q, kv_buf[pl.ds(0, i * step), :]), s], axis=1)
        state[rows, :] = state_of(*soft(s, one_buf[pl.ds(0, n), :]))
    o_mid, o_long = own_offsets(at_ref)
    qm_ref[...] = wide[pl.ds(o_mid, N_MID, stride=R_MID), :].astype(jnp.bfloat16)
    ql_ref[...] = wide[pl.ds(o_long, N_LONG, stride=R_LONG), :].astype(jnp.bfloat16)
    for i in range(N_MID // step):
        n = (i + 1) * step
        s = scores_of(qm_ref[pl.ds(i * step, step), :], kvm[:n])
        top, acc = soft(jnp.where(causal(step, n, i * step), s, NEGATIVE), with_ones(kvm[:n]))
        merge(state, pl.ds(o_mid + i * step * R_MID, step, stride=R_MID), top, acc)
    far = own_ref[...]
    s = scores_of(ql_ref[...], far)
    top, acc = soft(jnp.where(causal(N_LONG, N_LONG, 0), s, NEGATIVE), with_ones(far))
    merge(state, pl.ds(o_long, N_LONG, stride=R_LONG), top, acc)


def mid_part(state, qm, o_mid, pos, parts):
    step = 256
    ones = jnp.concatenate([with_ones(ref[...]) for _, ref in parts], axis=0)
    for i in range(N_MID // step):
        q = qm[pl.ds(i * step, step), :]
        pieces = []
        for d, ref in parts:
            before = jnp.bitwise_xor(pos, d) < pos
            pieces.append(scores_of(q, ref[...]) + jnp.where(before, 0.0, NEGATIVE))
        top, new = soft(jnp.concatenate(pieces, axis=1), ones)
        merge(state, pl.ds(o_mid + i * step * R_MID, step, stride=R_MID), top, new)


def long_part(state, ql, o_long, row, its_core, ref):
    every = ref[...].reshape(ZS * N_LONG, LANES)
    s = scores_of(ql[...], every)
    z = (lax.broadcasted_iota(jnp.int32, s.shape, 1) // N_LONG + Z_FIRST) % ZS
    before = 2 * z + its_core < row
    top, new = soft(jnp.where(before, s, NEGATIVE), with_ones(every))
    merge(state, pl.ds(o_long, N_LONG, stride=R_LONG), top, new)


def load_rows(src, first, dst, sems):
    count = sems.shape[0]
    part = dst.shape[0] // count
    pairs = [(src.at[pl.ds(first + i * part, part)], dst.at[pl.ds(i * part, part)]) for i in range(count)]
    return fetch(pairs, sems)


def near_kernel(at_ref, state_in, qm, m1, m2, w_hbm, state, w_ref, w_sems):
    loads = load_rows(w_hbm, 0, w_ref, w_sems)
    o_mid, _ = own_offsets(at_ref)
    mid_part(state, qm, o_mid, lax.rem(lax.axis_index("row"), MID_ROWS), ((1, m1), (2, m2)))
    for load in loads:
        load.wait()


def same_kernel(at_ref, state_in, qm, m3, ql, same, state):
    o_mid, o_long = own_offsets(at_ref)
    row = lax.axis_index("row")
    mid_part(state, qm, o_mid, lax.rem(row, MID_ROWS), ((3, m3),))
    long_part(state, ql, o_long, row, lax.rem(row, 2), same)


def last_kernel(at_ref, state_in, ql, other, w_hbm, out_ref, state, w_ref, w_sems):
    loads = load_rows(w_hbm, w_hbm.shape[0] - w_ref.shape[0], w_ref, w_sems)
    _, o_long = own_offsets(at_ref)
    row = lax.axis_index("row")
    long_part(state, ql, o_long, row, 1 - lax.rem(row, 2), other)
    low = low_lanes(HALF)
    for src in range(HEADS):
        done = []
        for half in range(2):
            a = state[pl.ds(src * BLOCK + half * HALF, HALF), :]
            done.append(a / a[:, :1])
        out_ref[slot(src)] = jnp.where(low, pltpu.roll(done[0], HD, 1), done[1]).astype(jnp.bfloat16)
    for load in loads:
        load.wait()


def project_kernel(got_ref, w0_ref, w1_ref, out_hbm, combined, tiles, sems):
    count, _, tile = tiles.shape
    for pair in range(HEADS // 2):
        a, b = got_ref[slot(2 * pair)], got_ref[slot(2 * pair + 1)]
        cols = pl.ds(pair * LANES, LANES)
        combined[:HALF, cols] = jnp.concatenate([a[:, :HD], b[:, :HD]], axis=1)
        combined[HALF:, cols] = jnp.concatenate([a[:, HD:], b[:, HD:]], axis=1)
    cut = w0_ref.shape[0]
    first, second = combined[:, :cut], combined[:, cut:]
    copies = []
    for i in range(count):
        cols = pl.ds(i * tile, tile)
        total = jnp.dot(first, w0_ref[:, cols], preferred_element_type=jnp.float32)
        total += jnp.dot(second, w1_ref[:, cols], preferred_element_type=jnp.float32)
        tiles[i] = total.astype(jnp.bfloat16)
        copies.append(pltpu.make_async_copy(tiles.at[i], out_hbm.at[:, cols], sems.at[i]))
        copies[-1].start()
    for copy in copies:
        copy.wait()


def xor_rows(x, d):
    return lax.ppermute(x, "row", [(i, i ^ d) for i in range(ROWS)])


CORES = [[2 * ((p + Z_FIRST) % ZS) + c for p in range(ZS)] for c in range(2)]
COLS = [[(p + COL_FIRST) % HEADS for p in range(HEADS)]]
bar = lax.optimization_barrier


def shards(queries, keys, values, mid_offsets, long_offsets, out_weight):
    f32, s32, bf16 = jnp.float32, jnp.int32, jnp.bfloat16
    width = queries.shape[1]
    depth, wide_out = out_weight.shape
    chunks = 4
    sent = call(
        pack_kernel,
        shape(HEADS, PACKED + NOTE, LANES),
        [HB] * 5,
        scratch=[pltpu.SMEM((HEADS,), s32)] * 2
        + [pltpu.VMEM((BLOCK, width), bf16)] * 3
        + [pltpu.VMEM((HEADS, PACKED + NOTE, LANES), bf16), DMA((2,)), DMA((chunks, 3)), DMA((chunks + 1,))],
        moved=1 << 20,
        out_specs=HB,
        limit=VMEM_MOST,
    )(mid_offsets, long_offsets, queries, keys, values)
    got = lax.all_to_all(sent, "col", 0, 0, axis_index_groups=COLS)
    kv_mid, own, at, far = call(
        select_kernel,
        (
            shape(N_MID, LANES),
            shape(N_LONG, LANES),
            shape(NOTE, LANES, dtype=f32),
            shape(ROWS // 2, N_LONG, LANES),
        ),
        [VM],
        scratch=[pltpu.VMEM((SEG, LANES), f32)],
        moved=1 << 20,
    )(got)
    m1 = xor_rows(kv_mid, 1)
    m2 = xor_rows(kv_mid, 2)
    same = lax.all_to_all(far, "row", 0, 0, axis_index_groups=CORES)
    state, q_mid, q_long = call(
        short_kernel,
        (shape(SEG, LANES, dtype=f32), shape(N_MID, LANES), shape(N_LONG, LANES)),
        [VM] * 4,
        scratch=[pltpu.VMEM((SEG, LANES), bf16)] * 2 + [pltpu.VMEM((SEG, LANES), f32)],
        flops=4 * SEG * SEG * LANES,
        moved=3 << 20,
        exps=SEG * SEG // 2,
    )(at, got, kv_mid, own)
    m1, m2, state = bar((m1, m2, state))
    m3 = xor_rows(m2, 1)
    early = depth * 3 // 8
    state, weight0 = call(
        near_kernel,
        (shape(SEG, LANES, dtype=f32), shape(early, wide_out)),
        [VM] * 5 + [HB],
        scratch=[DMA((1,))],
        flops=32 * 4 * N_MID * SEG * LANES,
        moved=2 << 20,
        exps=N_MID * SEG,
        aliases={1: 0},
        limit=VMEM_NEAR,
    )(at, state, q_mid, m1, m2, out_weight)
    same, m3, state = bar((same, m3, state))
    other = xor_rows(same, 1)
    state = call(
        same_kernel,
        shape(SEG, LANES, dtype=f32),
        [VM] * 6,
        flops=4 * N_MID * SEG * LANES,
        moved=2 << 20,
        exps=N_MID * SEG,
        aliases={1: 0},
    )(at, state, q_mid, m3, q_long, same)
    tile = 512
    count = wide_out // tile
    back, _, weight = call(
        last_kernel,
        (shape(HEADS, HALF, LANES), shape(SEG, LANES, dtype=f32), shape(depth - early, wide_out)),
        [VM] * 4 + [HB],
        scratch=[DMA((1,))],
        flops=4 * N_LONG * SEG * LANES,
        moved=4 << 20,
        exps=N_LONG * SEG,
        aliases={1: 1},
        limit=VMEM_LAST,
    )(at, state, q_long, other, out_weight)
    return call(
        project_kernel,
        shape(BLOCK, wide_out),
        [VM, VM, VM],
        scratch=[
            pltpu.VMEM((BLOCK, depth), bf16),
            pltpu.VMEM((count, BLOCK, tile), bf16),
            DMA((count,)),
        ],
        flops=2 * BLOCK * depth * wide_out,
        moved=2 * depth * wide_out,
        out_specs=HB,
    )(lax.all_to_all(back, "col", 0, 0, axis_index_groups=COLS), weight0, weight)


def solution(mesh):
    split = P(("row", "col"), None)
    return jax.shard_map(
        shards,
        mesh=mesh,
        in_specs=(split, split, split, P(), P(), P()),
        out_specs=split,
        check_vma=False,
    )
```

```python
import functools

import jax
import jax.numpy as jnp
from jax import lax
from jax.experimental import pallas as pl
from jax.experimental.pallas import tpu as pltpu
from jax.sharding import PartitionSpec as P

R_MID = 4
R_LONG = 16
HEADS = 16
HD = 64
LANES = 128
BLOCK = 128
SEG = 2048
HALF = BLOCK // 2
PACKED = BLOCK + HALF
NOTE = 16
ROWS = 16
MID_ROWS = 4
ZS = ROWS // 2
Z_FIRST = 6
COL_FIRST = 15
N_MID = SEG // R_MID
N_LONG = SEG // R_LONG
NEGATIVE = -1e30
SCALE = 0.125 * 1.4426950408889634
VMEM_LIMIT = 20 * 1024 * 1024
VMEM_LAST = 47 * 1024 * 1024
VMEM_NEAR = 49 * 1024 * 1024
VMEM_MOST = 60 * 1024 * 1024

VM = pl.BlockSpec(memory_space=pltpu.VMEM)
HB = pl.BlockSpec(memory_space=pl.ANY)
DMA = pltpu.SemaphoreType.DMA


def call(
    kernel, out_shape, in_specs, scratch=(), flops=0, moved=0, exps=0, out_specs=None, aliases=None, limit=VMEM_LIMIT
):
    return pl.pallas_call(
        kernel,
        out_shape=out_shape,
        in_specs=in_specs,
        out_specs=jax.tree.map(lambda _: VM, out_shape) if out_specs is None else out_specs,
        scratch_shapes=list(scratch),
        input_output_aliases=aliases or {},
        compiler_params=pltpu.CompilerParams(vmem_limit_bytes=limit),
        cost_estimate=pl.CostEstimate(flops=flops, bytes_accessed=moved, transcendentals=exps),
    )


def shape(*dims, dtype=jnp.bfloat16):
    return jax.ShapeDtypeStruct(dims, dtype)


def low_lanes(rows):
    return lax.broadcasted_iota(jnp.int32, (rows, LANES), 1) < HD


def fetch(pairs, sems):
    copies = [pltpu.make_async_copy(src, dst, sems.at[i]) for i, (src, dst) in enumerate(pairs)]
    for copy in copies:
        copy.start()
    return copies


def slot(col):
    return (col - COL_FIRST) % HEADS


def pack_kernel(
    mid_hbm, long_hbm, q_hbm, k_hbm, v_hbm, out_hbm,
    mid_ref, long_ref, q_ref, k_ref, v_ref, out_ref, at_sems, in_sems, out_sems,
):
    notes = fetch([(mid_hbm, mid_ref), (long_hbm, long_ref)], at_sems)
    chunks = in_sems.shape[0]
    heads = HEADS // chunks
    loads, stores = [], []
    for i in range(chunks):
        cols = pl.ds(i * heads * HD, heads * HD)
        pairs = [(src.at[:, cols], dst.at[:, cols]) for src, dst in ((k_hbm, k_ref), (v_hbm, v_ref), (q_hbm, q_ref))]
        loads.append(fetch(pairs, in_sems.at[i]))
    for copy in notes:
        copy.wait()
    for i in range(chunks):
        for copy in loads[i]:
            copy.wait()
        for head in range(i * heads, i * heads + heads):
            cols = pl.ds(head // 2 * LANES, LANES)
            lanes = slice(head % 2 * HD, head % 2 * HD + HD)
            q = q_ref[:, cols][:, lanes]
            out_ref[slot(head), :BLOCK] = jnp.concatenate([k_ref[:, cols][:, lanes], v_ref[:, cols][:, lanes]], axis=1)
            out_ref[slot(head), BLOCK:PACKED] = jnp.concatenate([q[:HALF], q[HALF:]], axis=1)
            note = jnp.where(low_lanes(NOTE), mid_ref[head].astype(jnp.float32), long_ref[head].astype(jnp.float32))
            out_ref[slot(head), PACKED:] = note.astype(jnp.bfloat16)
        slots = sorted(slot(head) for head in range(i * heads, i * heads + heads))
        runs = [[at for at in slots if at <= slots[0] + heads], [at for at in slots if at > slots[0] + heads]]
        for run in runs:
            if run:
                done = pl.ds(run[0], len(run))
                stores.append(pltpu.make_async_copy(out_ref.at[done], out_hbm.at[done], out_sems.at[len(stores)]))
                stores[-1].start()
    for copy in stores:
        copy.wait()


def select_kernel(got_ref, kvm_ref, own_ref, at_ref, far_ref, wide):
    at_ref[...] = got_ref[0, PACKED:].astype(jnp.float32)
    o_mid, o_long = own_offsets(at_ref)
    for src in range(HEADS):
        wide[pl.ds(src * BLOCK, BLOCK), :] = got_ref[slot(src), :BLOCK].astype(jnp.float32)
    far = wide[pl.ds(o_long, N_LONG, stride=R_LONG), :].astype(jnp.bfloat16)
    own_ref[...] = far
    for z in range(ROWS // 2):
        far_ref[z] = far
    kvm_ref[...] = wide[pl.ds(o_mid, N_MID, stride=R_MID), :].astype(jnp.bfloat16)


def own_offsets(at_ref):
    lane = lax.broadcasted_iota(jnp.int32, at_ref.shape, 1)
    at = at_ref[...].astype(jnp.int32)
    return [jnp.max(jnp.where(lane == where, at, 0)) for where in (0, LANES - 1)]


def scores_of(q, kv):
    return lax.dot_general(q, kv, (((1,), (1,)), ((), ())), preferred_element_type=jnp.float32)


def with_ones(kv):
    return jnp.where(low_lanes(kv.shape[0]), jnp.ones_like(kv), kv)


def soft(s, kv1):
    top = jnp.max(s, axis=1, keepdims=True)
    w = jnp.exp2((s - top) * SCALE).astype(jnp.bfloat16)
    return top, jnp.dot(w, kv1, preferred_element_type=jnp.float32)


def state_of(top, acc):
    lane = lax.broadcasted_iota(jnp.int32, acc.shape, 1)
    return jnp.where((lane >= HD // 2) & (lane < HD), top, acc)


def merge(state, rows, new_top, new_acc):
    old = state[rows, :]
    old_top = old[:, HD // 2 : HD // 2 + 1]
    best = jnp.maximum(old_top, new_top)
    acc = old * jnp.exp2((old_top - best) * SCALE) + new_acc * jnp.exp2((new_top - best) * SCALE)
    state[rows, :] = state_of(best, acc)


def causal(rows, cols, first):
    at = lax.broadcasted_iota(jnp.int32, (rows, cols), 0) + first
    return lax.broadcasted_iota(jnp.int32, (rows, cols), 1) <= at


def short_kernel(at_ref, got_ref, kvm, own_ref, state, qm_ref, ql_ref, kv_buf, one_buf, wide):
    for src in range(HEADS):
        rows = pl.ds(src * BLOCK, BLOCK)
        kv = got_ref[slot(src), :BLOCK]
        kv_buf[rows, :] = kv
        one_buf[rows, :] = with_ones(kv)
    step = 2 * BLOCK
    visible = causal(step, step, 0)
    low = low_lanes(HALF)
    zero = jnp.zeros((HALF, LANES), jnp.bfloat16)
    for i in range(SEG // step):
        parts = []
        for src in (2 * i, 2 * i + 1):
            packed = got_ref[slot(src), BLOCK:PACKED]
            parts.append(jnp.where(low, packed, zero))
            parts.append(jnp.where(low, jnp.concatenate([packed[:, HD:], packed[:, :HD]], axis=1), zero))
        q = jnp.concatenate(parts, axis=0)
        rows = pl.ds(i * step, step)
        wide[rows, :] = q.astype(jnp.float32)
        n = (i + 1) * step
        s = scores_of(q, kv_buf[rows, :])
        s = jnp.where(visible, s, NEGATIVE)
        if i:
            s = jnp.concatenate([scores_of(q, kv_buf[pl.ds(0, i * step), :]), s], axis=1)
        state[rows, :] = state_of(*soft(s, one_buf[pl.ds(0, n), :]))
    o_mid, o_long = own_offsets(at_ref)
    qm_ref[...] = wide[pl.ds(o_mid, N_MID, stride=R_MID), :].astype(jnp.bfloat16)
    ql_ref[...] = wide[pl.ds(o_long, N_LONG, stride=R_LONG), :].astype(jnp.bfloat16)
    for i in range(N_MID // step):
        n = (i + 1) * step
        s = scores_of(qm_ref[pl.ds(i * step, step), :], kvm[:n])
        top, acc = soft(jnp.where(causal(step, n, i * step), s, NEGATIVE), with_ones(kvm[:n]))
        merge(state, pl.ds(o_mid + i * step * R_MID, step, stride=R_MID), top, acc)
    far = own_ref[...]
    s = scores_of(ql_ref[...], far)
    top, acc = soft(jnp.where(causal(N_LONG, N_LONG, 0), s, NEGATIVE), with_ones(far))
    merge(state, pl.ds(o_long, N_LONG, stride=R_LONG), top, acc)


def mid_part(state, qm, o_mid, pos, parts):
    step = 256
    ones = jnp.concatenate([with_ones(ref[...]) for _, ref in parts], axis=0)
    for i in range(N_MID // step):
        q = qm[pl.ds(i * step, step), :]
        pieces = []
        for d, ref in parts:
            before = jnp.bitwise_xor(pos, d) < pos
            pieces.append(scores_of(q, ref[...]) + jnp.where(before, 0.0, NEGATIVE))
        top, new = soft(jnp.concatenate(pieces, axis=1), ones)
        merge(state, pl.ds(o_mid + i * step * R_MID, step, stride=R_MID), top, new)


def long_part(state, ql, o_long, row, its_core, ref):
    every = ref[...].reshape(ZS * N_LONG, LANES)
    s = scores_of(ql[...], every)
    z = (lax.broadcasted_iota(jnp.int32, s.shape, 1) // N_LONG + Z_FIRST) % ZS
    before = 2 * z + its_core < row
    top, new = soft(jnp.where(before, s, NEGATIVE), with_ones(every))
    merge(state, pl.ds(o_long, N_LONG, stride=R_LONG), top, new)


def load_rows(src, first, dst, sems):
    count = sems.shape[0]
    part = dst.shape[0] // count
    pairs = [(src.at[pl.ds(first + i * part, part)], dst.at[pl.ds(i * part, part)]) for i in range(count)]
    return fetch(pairs, sems)


def near_kernel(at_ref, state_in, qm, m1, m2, w_hbm, state, w_ref, w_sems):
    loads = load_rows(w_hbm, 0, w_ref, w_sems)
    o_mid, _ = own_offsets(at_ref)
    mid_part(state, qm, o_mid, lax.rem(lax.axis_index("row"), MID_ROWS), ((1, m1), (2, m2)))
    for load in loads:
        load.wait()


def same_kernel(at_ref, state_in, qm, m3, ql, same, state):
    o_mid, o_long = own_offsets(at_ref)
    row = lax.axis_index("row")
    mid_part(state, qm, o_mid, lax.rem(row, MID_ROWS), ((3, m3),))
    long_part(state, ql, o_long, row, lax.rem(row, 2), same)


def last_kernel(at_ref, state_in, ql, other, w_hbm, out_ref, state, w_ref, w_sems):
    loads = load_rows(w_hbm, w_hbm.shape[0] - w_ref.shape[0], w_ref, w_sems)
    _, o_long = own_offsets(at_ref)
    row = lax.axis_index("row")
    long_part(state, ql, o_long, row, 1 - lax.rem(row, 2), other)
    low = low_lanes(HALF)
    for src in range(HEADS):
        done = []
        for half in range(2):
            a = state[pl.ds(src * BLOCK + half * HALF, HALF), :]
            done.append(a / a[:, :1])
        out_ref[slot(src)] = jnp.where(low, pltpu.roll(done[0], HD, 1), done[1]).astype(jnp.bfloat16)
    for load in loads:
        load.wait()


def project_kernel(got_ref, w0_ref, w1_ref, out_hbm, combined, tiles, sems):
    count, _, tile = tiles.shape
    for pair in range(HEADS // 2):
        a, b = got_ref[slot(2 * pair)], got_ref[slot(2 * pair + 1)]
        cols = pl.ds(pair * LANES, LANES)
        combined[:HALF, cols] = jnp.concatenate([a[:, :HD], b[:, :HD]], axis=1)
        combined[HALF:, cols] = jnp.concatenate([a[:, HD:], b[:, HD:]], axis=1)
    cut = w0_ref.shape[0]
    first, second = combined[:, :cut], combined[:, cut:]
    copies = []
    for i in range(count):
        cols = pl.ds(i * tile, tile)
        total = jnp.dot(first, w0_ref[:, cols], preferred_element_type=jnp.float32)
        total += jnp.dot(second, w1_ref[:, cols], preferred_element_type=jnp.float32)
        tiles[i] = total.astype(jnp.bfloat16)
        copies.append(pltpu.make_async_copy(tiles.at[i], out_hbm.at[:, cols], sems.at[i]))
        copies[-1].start()
    for copy in copies:
        copy.wait()


def xor_rows(x, d):
    return lax.ppermute(x, "row", [(i, i ^ d) for i in range(ROWS)])


CORES = [[2 * ((p + Z_FIRST) % ZS) + c for p in range(ZS)] for c in range(2)]
COLS = [[(p + COL_FIRST) % HEADS for p in range(HEADS)]]
bar = lax.optimization_barrier


def shards(queries, keys, values, mid_offsets, long_offsets, out_weight):
    f32, s32, bf16 = jnp.float32, jnp.int32, jnp.bfloat16
    width = queries.shape[1]
    depth, wide_out = out_weight.shape
    chunks = 4
    sent = call(
        pack_kernel,
        shape(HEADS, PACKED + NOTE, LANES),
        [HB] * 5,
        scratch=[pltpu.SMEM((HEADS,), s32)] * 2
        + [pltpu.VMEM((BLOCK, width), bf16)] * 3
        + [pltpu.VMEM((HEADS, PACKED + NOTE, LANES), bf16), DMA((2,)), DMA((chunks, 3)), DMA((chunks + 1,))],
        moved=1 << 20,
        out_specs=HB,
        limit=VMEM_MOST,
    )(mid_offsets, long_offsets, queries, keys, values)
    got = lax.all_to_all(sent, "col", 0, 0, axis_index_groups=COLS)
    kv_mid, own, at, far = call(
        select_kernel,
        (
            shape(N_MID, LANES),
            shape(N_LONG, LANES),
            shape(NOTE, LANES, dtype=f32),
            shape(ROWS // 2, N_LONG, LANES),
        ),
        [VM],
        scratch=[pltpu.VMEM((SEG, LANES), f32)],
        moved=1 << 20,
    )(got)
    m1 = xor_rows(kv_mid, 1)
    m2 = xor_rows(kv_mid, 2)
    same = lax.all_to_all(far, "row", 0, 0, axis_index_groups=CORES)
    state, q_mid, q_long = call(
        short_kernel,
        (shape(SEG, LANES, dtype=f32), shape(N_MID, LANES), shape(N_LONG, LANES)),
        [VM] * 4,
        scratch=[pltpu.VMEM((SEG, LANES), bf16)] * 2 + [pltpu.VMEM((SEG, LANES), f32)],
        flops=4 * SEG * SEG * LANES,
        moved=3 << 20,
        exps=SEG * SEG // 2,
    )(at, got, kv_mid, own)
    m1, m2, state = bar((m1, m2, state))
    m3 = xor_rows(m2, 1)
    early = depth * 3 // 8
    state, weight0 = call(
        near_kernel,
        (shape(SEG, LANES, dtype=f32), shape(early, wide_out)),
        [VM] * 5 + [HB],
        scratch=[DMA((1,))],
        flops=32 * 4 * N_MID * SEG * LANES,
        moved=2 << 20,
        exps=N_MID * SEG,
        aliases={1: 0},
        limit=VMEM_NEAR,
    )(at, state, q_mid, m1, m2, out_weight)
    same, m3, state = bar((same, m3, state))
    other = xor_rows(same, 1)
    state = call(
        same_kernel,
        shape(SEG, LANES, dtype=f32),
        [VM] * 6,
        flops=4 * N_MID * SEG * LANES,
        moved=2 << 20,
        exps=N_MID * SEG,
        aliases={1: 0},
    )(at, state, q_mid, m3, q_long, same)
    tile = 512
    count = wide_out // tile
    back, _, weight = call(
        last_kernel,
        (shape(HEADS, HALF, LANES), shape(SEG, LANES, dtype=f32), shape(depth - early, wide_out)),
        [VM] * 4 + [HB],
        scratch=[DMA((1,))],
        flops=4 * N_LONG * SEG * LANES,
        moved=4 << 20,
        exps=N_LONG * SEG,
        aliases={1: 1},
        limit=VMEM_LAST,
    )(at, state, q_long, other, out_weight)
    return call(
        project_kernel,
        shape(BLOCK, wide_out),
        [VM, VM, VM],
        scratch=[
            pltpu.VMEM((BLOCK, depth), bf16),
            pltpu.VMEM((count, BLOCK, tile), bf16),
            DMA((count,)),
        ],
        flops=2 * BLOCK * depth * wide_out,
        moved=2 * depth * wide_out,
        out_specs=HB,
    )(lax.all_to_all(back, "col", 0, 0, axis_index_groups=COLS), weight0, weight)


def solution(mesh):
    split = P(("row", "col"), None)
    return jax.shard_map(
        shards,
        mesh=mesh,
        in_specs=(split, split, split, P(), P(), P()),
        out_specs=split,
        check_vma=False,
    )
```

```python
import functools

import jax
import jax.numpy as jnp
from jax import lax
from jax.experimental import pallas as pl
from jax.experimental.pallas import tpu as pltpu
from jax.sharding import PartitionSpec as P

R_MID = 4
R_LONG = 16
HEADS = 16
HD = 64
LANES = 128
BLOCK = 128
SEG = 2048
HALF = BLOCK // 2
PACKED = BLOCK + HALF
NOTE = 16
ROWS = 16
MID_ROWS = 4
ZS = ROWS // 2
Z_FIRST = 5
COL_FIRST = 15
N_MID = SEG // R_MID
N_LONG = SEG // R_LONG
NEGATIVE = -1e30
SCALE = 0.125 * 1.4426950408889634
VMEM_LIMIT = 20 * 1024 * 1024
VMEM_LAST = 47 * 1024 * 1024
VMEM_NEAR = 49 * 1024 * 1024
VMEM_PROJECT = 48 * 1024 * 1024
CUTS = (768, 1792)
VMEM_MOST = 60 * 1024 * 1024

VM = pl.BlockSpec(memory_space=pltpu.VMEM)
HB = pl.BlockSpec(memory_space=pl.ANY)
DMA = pltpu.SemaphoreType.DMA


def call(
    kernel, out_shape, in_specs, scratch=(), flops=0, moved=0, exps=0, out_specs=None, aliases=None, limit=VMEM_LIMIT
):
    return pl.pallas_call(
        kernel,
        out_shape=out_shape,
        in_specs=in_specs,
        out_specs=jax.tree.map(lambda _: VM, out_shape) if out_specs is None else out_specs,
        scratch_shapes=list(scratch),
        input_output_aliases=aliases or {},
        compiler_params=pltpu.CompilerParams(vmem_limit_bytes=limit),
        cost_estimate=pl.CostEstimate(flops=flops, bytes_accessed=moved, transcendentals=exps),
    )


def shape(*dims, dtype=jnp.bfloat16):
    return jax.ShapeDtypeStruct(dims, dtype)


def low_lanes(rows):
    return lax.broadcasted_iota(jnp.int32, (rows, LANES), 1) < HD


def fetch(pairs, sems):
    copies = [pltpu.make_async_copy(src, dst, sems.at[i]) for i, (src, dst) in enumerate(pairs)]
    for copy in copies:
        copy.start()
    return copies


def slot(col):
    return (col - COL_FIRST) % HEADS


def pack_kernel(
    mid_hbm, long_hbm, q_hbm, k_hbm, v_hbm, out_hbm,
    mid_ref, long_ref, q_ref, k_ref, v_ref, out_ref, at_sems, in_sems, out_sems,
):
    notes = fetch([(mid_hbm, mid_ref), (long_hbm, long_ref)], at_sems)
    chunks = in_sems.shape[0]
    heads = HEADS // chunks
    loads, stores = [], []
    for i in range(chunks):
        cols = pl.ds(i * heads * HD, heads * HD)
        pairs = [(src.at[:, cols], dst.at[:, cols]) for src, dst in ((k_hbm, k_ref), (v_hbm, v_ref), (q_hbm, q_ref))]
        loads.append(fetch(pairs, in_sems.at[i]))
    for copy in notes:
        copy.wait()
    for i in range(chunks):
        for copy in loads[i]:
            copy.wait()
        for head in range(i * heads, i * heads + heads):
            cols = pl.ds(head // 2 * LANES, LANES)
            lanes = slice(head % 2 * HD, head % 2 * HD + HD)
            q = q_ref[:, cols][:, lanes]
            out_ref[slot(head), :BLOCK] = jnp.concatenate([k_ref[:, cols][:, lanes], v_ref[:, cols][:, lanes]], axis=1)
            out_ref[slot(head), BLOCK:PACKED] = jnp.concatenate([q[:HALF], q[HALF:]], axis=1)
            note = jnp.where(low_lanes(NOTE), mid_ref[head].astype(jnp.float32), long_ref[head].astype(jnp.float32))
            out_ref[slot(head), PACKED:] = note.astype(jnp.bfloat16)
        slots = sorted(slot(head) for head in range(i * heads, i * heads + heads))
        runs = [[at for at in slots if at <= slots[0] + heads], [at for at in slots if at > slots[0] + heads]]
        for run in runs:
            if run:
                done = pl.ds(run[0], len(run))
                stores.append(pltpu.make_async_copy(out_ref.at[done], out_hbm.at[done], out_sems.at[len(stores)]))
                stores[-1].start()
    for copy in stores:
        copy.wait()


def select_kernel(got_ref, kvm_ref, own_ref, at_ref, far_ref, wide):
    at_ref[...] = got_ref[0, PACKED:].astype(jnp.float32)
    o_mid, o_long = own_offsets(at_ref)
    for src in range(HEADS):
        wide[pl.ds(src * BLOCK, BLOCK), :] = got_ref[slot(src), :BLOCK].astype(jnp.float32)
    far = wide[pl.ds(o_long, N_LONG, stride=R_LONG), :].astype(jnp.bfloat16)
    own_ref[...] = far
    for z in range(ROWS // 2):
        far_ref[z] = far
    kvm_ref[...] = wide[pl.ds(o_mid, N_MID, stride=R_MID), :].astype(jnp.bfloat16)


def own_offsets(at_ref):
    lane = lax.broadcasted_iota(jnp.int32, at_ref.shape, 1)
    at = at_ref[...].astype(jnp.int32)
    return [jnp.max(jnp.where(lane == where, at, 0)) for where in (0, LANES - 1)]


def scores_of(q, kv):
    return lax.dot_general(q, kv, (((1,), (1,)), ((), ())), preferred_element_type=jnp.float32)


def with_ones(kv):
    return jnp.where(low_lanes(kv.shape[0]), jnp.ones_like(kv), kv)


def soft(s, kv1):
    top = jnp.max(s, axis=1, keepdims=True)
    w = jnp.exp2((s - top) * SCALE).astype(jnp.bfloat16)
    return top, jnp.dot(w, kv1, preferred_element_type=jnp.float32)


def state_of(top, acc):
    lane = lax.broadcasted_iota(jnp.int32, acc.shape, 1)
    return jnp.where((lane >= HD // 2) & (lane < HD), top, acc)


def merge(state, rows, new_top, new_acc):
    old = state[rows, :]
    old_top = old[:, HD // 2 : HD // 2 + 1]
    best = jnp.maximum(old_top, new_top)
    acc = old * jnp.exp2((old_top - best) * SCALE) + new_acc * jnp.exp2((new_top - best) * SCALE)
    state[rows, :] = state_of(best, acc)


def causal(rows, cols, first):
    at = lax.broadcasted_iota(jnp.int32, (rows, cols), 0) + first
    return lax.broadcasted_iota(jnp.int32, (rows, cols), 1) <= at


def short_kernel(at_ref, got_ref, kvm, own_ref, state, qm_ref, ql_ref, kv_buf, one_buf, wide):
    for src in range(HEADS):
        rows = pl.ds(src * BLOCK, BLOCK)
        kv = got_ref[slot(src), :BLOCK]
        kv_buf[rows, :] = kv
        one_buf[rows, :] = with_ones(kv)
    step = 2 * BLOCK
    visible = causal(step, step, 0)
    low = low_lanes(HALF)
    zero = jnp.zeros((HALF, LANES), jnp.bfloat16)
    for i in range(SEG // step):
        parts = []
        for src in (2 * i, 2 * i + 1):
            packed = got_ref[slot(src), BLOCK:PACKED]
            parts.append(jnp.where(low, packed, zero))
            parts.append(jnp.where(low, jnp.concatenate([packed[:, HD:], packed[:, :HD]], axis=1), zero))
        q = jnp.concatenate(parts, axis=0)
        rows = pl.ds(i * step, step)
        wide[rows, :] = q.astype(jnp.float32)
        n = (i + 1) * step
        s = scores_of(q, kv_buf[rows, :])
        s = jnp.where(visible, s, NEGATIVE)
        if i:
            s = jnp.concatenate([scores_of(q, kv_buf[pl.ds(0, i * step), :]), s], axis=1)
        state[rows, :] = state_of(*soft(s, one_buf[pl.ds(0, n), :]))
    o_mid, o_long = own_offsets(at_ref)
    qm_ref[...] = wide[pl.ds(o_mid, N_MID, stride=R_MID), :].astype(jnp.bfloat16)
    ql_ref[...] = wide[pl.ds(o_long, N_LONG, stride=R_LONG), :].astype(jnp.bfloat16)
    for i in range(N_MID // step):
        n = (i + 1) * step
        s = scores_of(qm_ref[pl.ds(i * step, step), :], kvm[:n])
        top, acc = soft(jnp.where(causal(step, n, i * step), s, NEGATIVE), with_ones(kvm[:n]))
        merge(state, pl.ds(o_mid + i * step * R_MID, step, stride=R_MID), top, acc)
    far = own_ref[...]
    s = scores_of(ql_ref[...], far)
    top, acc = soft(jnp.where(causal(N_LONG, N_LONG, 0), s, NEGATIVE), with_ones(far))
    merge(state, pl.ds(o_long, N_LONG, stride=R_LONG), top, acc)


def mid_part(state, qm, o_mid, pos, parts):
    step = 256
    ones = jnp.concatenate([with_ones(ref[...]) for _, ref in parts], axis=0)
    for i in range(N_MID // step):
        q = qm[pl.ds(i * step, step), :]
        pieces = []
        for d, ref in parts:
            before = jnp.bitwise_xor(pos, d) < pos
            pieces.append(scores_of(q, ref[...]) + jnp.where(before, 0.0, NEGATIVE))
        top, new = soft(jnp.concatenate(pieces, axis=1), ones)
        merge(state, pl.ds(o_mid + i * step * R_MID, step, stride=R_MID), top, new)


def long_part(state, ql, o_long, row, its_core, ref):
    every = ref[...].reshape(ZS * N_LONG, LANES)
    s = scores_of(ql[...], every)
    z = (lax.broadcasted_iota(jnp.int32, s.shape, 1) // N_LONG + Z_FIRST) % ZS
    before = 2 * z + its_core < row
    top, new = soft(jnp.where(before, s, NEGATIVE), with_ones(every))
    merge(state, pl.ds(o_long, N_LONG, stride=R_LONG), top, new)


def load_cols(src, first, dst, sem):
    load = pltpu.make_async_copy(src.at[:, pl.ds(first, dst.shape[1])], dst, sem)
    load.start()
    return load


def near_kernel(at_ref, state_in, qm, m1, m2, w_hbm, state, w_ref, w_sem):
    load = load_cols(w_hbm, 0, w_ref, w_sem)
    o_mid, _ = own_offsets(at_ref)
    mid_part(state, qm, o_mid, lax.rem(lax.axis_index("row"), MID_ROWS), ((1, m1), (2, m2)))
    load.wait()


def same_kernel(at_ref, state_in, qm, m3, ql, same, state):
    o_mid, o_long = own_offsets(at_ref)
    row = lax.axis_index("row")
    mid_part(state, qm, o_mid, lax.rem(row, MID_ROWS), ((3, m3),))
    long_part(state, ql, o_long, row, lax.rem(row, 2), same)


def last_kernel(at_ref, state_in, ql, other, w_hbm, out_ref, state, w_ref, w_sem):
    load = load_cols(w_hbm, CUTS[0], w_ref, w_sem)
    _, o_long = own_offsets(at_ref)
    row = lax.axis_index("row")
    long_part(state, ql, o_long, row, 1 - lax.rem(row, 2), other)
    low = low_lanes(HALF)
    for src in range(HEADS):
        done = []
        for half in range(2):
            a = state[pl.ds(src * BLOCK + half * HALF, HALF), :]
            done.append(a / a[:, :1])
        out_ref[slot(src)] = jnp.where(low, pltpu.roll(done[0], HD, 1), done[1]).astype(jnp.bfloat16)
    load.wait()


def project_kernel(got_ref, w0_ref, w1_ref, w_hbm, out_hbm, combined, rest, out_ref, w_sem, sems):
    load = load_cols(w_hbm, CUTS[1], rest, w_sem)
    for pair in range(HEADS // 2):
        a, b = got_ref[slot(2 * pair)], got_ref[slot(2 * pair + 1)]
        cols = pl.ds(pair * LANES, LANES)
        combined[:HALF, cols] = jnp.concatenate([a[:, :HD], b[:, :HD]], axis=1)
        combined[HALF:, cols] = jnp.concatenate([a[:, HD:], b[:, HD:]], axis=1)
    rows = combined[...]
    tile = w1_ref.shape[1] // 2
    pieces = [(0, w0_ref, 0, CUTS[0]), (CUTS[0], w1_ref, 0, tile), (CUTS[0] + tile, w1_ref, tile, tile)]
    pieces.append((CUTS[1], rest, 0, rest.shape[1]))
    copies = []
    for first, ref, at, width in pieces:
        if ref is rest:
            load.wait()
        cols = pl.ds(first, width)
        total = jnp.dot(rows, ref[:, pl.ds(at, width)], preferred_element_type=jnp.float32)
        out_ref[:, cols] = total.astype(jnp.bfloat16)
        copies.append(pltpu.make_async_copy(out_ref.at[:, cols], out_hbm.at[:, cols], sems.at[len(copies)]))
        copies[-1].start()
    for copy in copies:
        copy.wait()


def xor_rows(x, d):
    return lax.ppermute(x, "row", [(i, i ^ d) for i in range(ROWS)])


CORES = [[2 * ((p + Z_FIRST) % ZS) + c for p in range(ZS)] for c in range(2)]
COLS = [[(p + COL_FIRST) % HEADS for p in range(HEADS)]]
bar = lax.optimization_barrier


def shards(queries, keys, values, mid_offsets, long_offsets, out_weight):
    f32, s32, bf16 = jnp.float32, jnp.int32, jnp.bfloat16
    width = queries.shape[1]
    depth, wide_out = out_weight.shape
    chunks = 4
    sent = call(
        pack_kernel,
        shape(HEADS, PACKED + NOTE, LANES),
        [HB] * 5,
        scratch=[pltpu.SMEM((HEADS,), s32)] * 2
        + [pltpu.VMEM((BLOCK, width), bf16)] * 3
        + [pltpu.VMEM((HEADS, PACKED + NOTE, LANES), bf16), DMA((2,)), DMA((chunks, 3)), DMA((chunks + 1,))],
        moved=1 << 20,
        out_specs=HB,
        limit=VMEM_MOST,
    )(mid_offsets, long_offsets, queries, keys, values)
    got = lax.all_to_all(sent, "col", 0, 0, axis_index_groups=COLS)
    kv_mid, own, at, far = call(
        select_kernel,
        (
            shape(N_MID, LANES),
            shape(N_LONG, LANES),
            shape(NOTE, LANES, dtype=f32),
            shape(ROWS // 2, N_LONG, LANES),
        ),
        [VM],
        scratch=[pltpu.VMEM((SEG, LANES), f32)],
        moved=1 << 20,
    )(got)
    m1 = xor_rows(kv_mid, 1)
    m2 = xor_rows(kv_mid, 2)
    same = lax.all_to_all(far, "row", 0, 0, axis_index_groups=CORES)
    state, q_mid, q_long = call(
        short_kernel,
        (shape(SEG, LANES, dtype=f32), shape(N_MID, LANES), shape(N_LONG, LANES)),
        [VM] * 4,
        scratch=[pltpu.VMEM((SEG, LANES), bf16)] * 2 + [pltpu.VMEM((SEG, LANES), f32)],
        flops=4 * SEG * SEG * LANES,
        moved=3 << 20,
        exps=SEG * SEG // 2,
    )(at, got, kv_mid, own)
    m1, m2, state = bar((m1, m2, state))
    m3 = xor_rows(m2, 1)
    state, weight0 = call(
        near_kernel,
        (shape(SEG, LANES, dtype=f32), shape(depth, CUTS[0])),
        [VM] * 5 + [HB],
        scratch=[DMA],
        flops=32 * 4 * N_MID * SEG * LANES,
        moved=2 << 20,
        exps=N_MID * SEG,
        aliases={1: 0},
        limit=VMEM_NEAR,
    )(at, state, q_mid, m1, m2, out_weight)
    same, m3, state = bar((same, m3, state))
    other = xor_rows(same, 1)
    state = call(
        same_kernel,
        shape(SEG, LANES, dtype=f32),
        [VM] * 6,
        flops=4 * N_MID * SEG * LANES,
        moved=2 << 20,
        exps=N_MID * SEG,
        aliases={1: 0},
    )(at, state, q_mid, m3, q_long, same)
    back, _, weight = call(
        last_kernel,
        (shape(HEADS, HALF, LANES), shape(SEG, LANES, dtype=f32), shape(depth, CUTS[1] - CUTS[0])),
        [VM] * 4 + [HB],
        scratch=[DMA],
        flops=4 * N_LONG * SEG * LANES,
        moved=4 << 20,
        exps=N_LONG * SEG,
        aliases={1: 1},
        limit=VMEM_LAST,
    )(at, state, q_long, other, out_weight)
    return call(
        project_kernel,
        shape(BLOCK, wide_out),
        [VM, VM, VM, HB],
        scratch=[
            pltpu.VMEM((BLOCK, depth), bf16),
            pltpu.VMEM((depth, wide_out - CUTS[1]), bf16),
            pltpu.VMEM((BLOCK, wide_out), bf16),
            DMA,
            DMA((4,)),
        ],
        flops=2 * BLOCK * depth * wide_out,
        moved=2 * depth * wide_out,
        out_specs=HB,
        limit=VMEM_PROJECT,
    )(lax.all_to_all(back, "col", 0, 0, axis_index_groups=COLS), weight0, weight, out_weight)


def solution(mesh):
    split = P(("row", "col"), None)
    return jax.shard_map(
        shards,
        mesh=mesh,
        in_specs=(split, split, split, P(), P(), P()),
        out_specs=split,
        check_vma=False,
    )
```

```python
import functools

import jax
import jax.numpy as jnp
from jax import lax
from jax.experimental import pallas as pl
from jax.experimental.pallas import tpu as pltpu
from jax.sharding import PartitionSpec as P

R_MID = 4
R_LONG = 16
HEADS = 16
HD = 64
LANES = 128
BLOCK = 128
SEG = 2048
HALF = BLOCK // 2
PACKED = BLOCK + HALF
NOTE = 16
ROWS = 16
MID_ROWS = 4
ZS = ROWS // 2
Z_FIRST = 5
COL_FIRST = 15
N_MID = SEG // R_MID
N_LONG = SEG // R_LONG
NEGATIVE = -1e30
SCALE = 0.125 * 1.4426950408889634
VMEM_LIMIT = 20 * 1024 * 1024
VMEM_LAST = 47 * 1024 * 1024
VMEM_NEAR = 49 * 1024 * 1024
VMEM_MOST = 60 * 1024 * 1024

VM = pl.BlockSpec(memory_space=pltpu.VMEM)
HB = pl.BlockSpec(memory_space=pl.ANY)
DMA = pltpu.SemaphoreType.DMA


def call(
    kernel, out_shape, in_specs, scratch=(), flops=0, moved=0, exps=0, out_specs=None, aliases=None, limit=VMEM_LIMIT
):
    return pl.pallas_call(
        kernel,
        out_shape=out_shape,
        in_specs=in_specs,
        out_specs=jax.tree.map(lambda _: VM, out_shape) if out_specs is None else out_specs,
        scratch_shapes=list(scratch),
        input_output_aliases=aliases or {},
        compiler_params=pltpu.CompilerParams(vmem_limit_bytes=limit),
        cost_estimate=pl.CostEstimate(flops=flops, bytes_accessed=moved, transcendentals=exps),
    )


def shape(*dims, dtype=jnp.bfloat16):
    return jax.ShapeDtypeStruct(dims, dtype)


def low_lanes(rows):
    return lax.broadcasted_iota(jnp.int32, (rows, LANES), 1) < HD


def fetch(pairs, sems):
    copies = [pltpu.make_async_copy(src, dst, sems.at[i]) for i, (src, dst) in enumerate(pairs)]
    for copy in copies:
        copy.start()
    return copies


def slot(col):
    return (col - COL_FIRST) % HEADS


def pack_kernel(
    mid_hbm, long_hbm, q_hbm, k_hbm, v_hbm, out_hbm,
    mid_ref, long_ref, q_ref, k_ref, v_ref, out_ref, at_sems, in_sems, out_sems,
):
    notes = fetch([(mid_hbm, mid_ref), (long_hbm, long_ref)], at_sems)
    chunks = in_sems.shape[0]
    heads = HEADS // chunks
    loads, stores = [], []
    for i in range(chunks):
        cols = pl.ds(i * heads * HD, heads * HD)
        pairs = [(src.at[:, cols], dst.at[:, cols]) for src, dst in ((k_hbm, k_ref), (v_hbm, v_ref), (q_hbm, q_ref))]
        loads.append(fetch(pairs, in_sems.at[i]))
    for copy in notes:
        copy.wait()
    for i in range(chunks):
        for copy in loads[i]:
            copy.wait()
        for head in range(i * heads, i * heads + heads):
            cols = pl.ds(head // 2 * LANES, LANES)
            lanes = slice(head % 2 * HD, head % 2 * HD + HD)
            q = q_ref[:, cols][:, lanes]
            out_ref[slot(head), :BLOCK] = jnp.concatenate([k_ref[:, cols][:, lanes], v_ref[:, cols][:, lanes]], axis=1)
            out_ref[slot(head), BLOCK:PACKED] = jnp.concatenate([q[:HALF], q[HALF:]], axis=1)
            note = jnp.where(low_lanes(NOTE), mid_ref[head].astype(jnp.float32), long_ref[head].astype(jnp.float32))
            out_ref[slot(head), PACKED:] = note.astype(jnp.bfloat16)
        slots = sorted(slot(head) for head in range(i * heads, i * heads + heads))
        runs = [[at for at in slots if at <= slots[0] + heads], [at for at in slots if at > slots[0] + heads]]
        for run in runs:
            if run:
                done = pl.ds(run[0], len(run))
                stores.append(pltpu.make_async_copy(out_ref.at[done], out_hbm.at[done], out_sems.at[len(stores)]))
                stores[-1].start()
    for copy in stores:
        copy.wait()


def select_kernel(got_ref, kvm_ref, own_ref, at_ref, far_ref, wide):
    at_ref[...] = got_ref[0, PACKED:].astype(jnp.float32)
    o_mid, o_long = own_offsets(at_ref)
    for src in range(HEADS):
        wide[pl.ds(src * BLOCK, BLOCK), :] = got_ref[slot(src), :BLOCK].astype(jnp.float32)
    far = wide[pl.ds(o_long, N_LONG, stride=R_LONG), :].astype(jnp.bfloat16)
    own_ref[...] = far
    for z in range(ROWS // 2):
        far_ref[z] = far
    kvm_ref[...] = wide[pl.ds(o_mid, N_MID, stride=R_MID), :].astype(jnp.bfloat16)


def own_offsets(at_ref):
    lane = lax.broadcasted_iota(jnp.int32, at_ref.shape, 1)
    at = at_ref[...].astype(jnp.int32)
    return [jnp.max(jnp.where(lane == where, at, 0)) for where in (0, LANES - 1)]


def scores_of(q, kv):
    return lax.dot_general(q, kv, (((1,), (1,)), ((), ())), preferred_element_type=jnp.float32)


def with_ones(kv):
    return jnp.where(low_lanes(kv.shape[0]), jnp.ones_like(kv), kv)


def soft(s, kv1):
    top = jnp.max(s, axis=1, keepdims=True)
    w = jnp.exp2((s - top) * SCALE).astype(jnp.bfloat16)
    return top, jnp.dot(w, kv1, preferred_element_type=jnp.float32)


def state_of(top, acc):
    lane = lax.broadcasted_iota(jnp.int32, acc.shape, 1)
    return jnp.where((lane >= HD // 2) & (lane < HD), top, acc)


def merge(state, rows, new_top, new_acc):
    old = state[rows, :]
    old_top = old[:, HD // 2 : HD // 2 + 1]
    best = jnp.maximum(old_top, new_top)
    acc = old * jnp.exp2((old_top - best) * SCALE) + new_acc * jnp.exp2((new_top - best) * SCALE)
    state[rows, :] = state_of(best, acc)


def causal(rows, cols, first):
    at = lax.broadcasted_iota(jnp.int32, (rows, cols), 0) + first
    return lax.broadcasted_iota(jnp.int32, (rows, cols), 1) <= at


def short_kernel(at_ref, got_ref, kvm, own_ref, state, qm_ref, ql_ref, kv_buf, one_buf, wide):
    for src in range(HEADS):
        rows = pl.ds(src * BLOCK, BLOCK)
        kv = got_ref[slot(src), :BLOCK]
        kv_buf[rows, :] = kv
        one_buf[rows, :] = with_ones(kv)
    blocks = 4
    step = blocks * BLOCK
    visible = causal(step, step, 0)
    low = low_lanes(HALF)
    zero = jnp.zeros((HALF, LANES), jnp.bfloat16)
    for i in range(SEG // step):
        parts = []
        for src in range(blocks * i, blocks * i + blocks):
            packed = got_ref[slot(src), BLOCK:PACKED]
            parts.append(jnp.where(low, packed, zero))
            parts.append(jnp.where(low, jnp.concatenate([packed[:, HD:], packed[:, :HD]], axis=1), zero))
        q = jnp.concatenate(parts, axis=0)
        rows = pl.ds(i * step, step)
        wide[rows, :] = q.astype(jnp.float32)
        n = (i + 1) * step
        s = scores_of(q, kv_buf[rows, :])
        s = jnp.where(visible, s, NEGATIVE)
        if i:
            s = jnp.concatenate([scores_of(q, kv_buf[pl.ds(0, i * step), :]), s], axis=1)
        state[rows, :] = state_of(*soft(s, one_buf[pl.ds(0, n), :]))
    o_mid, o_long = own_offsets(at_ref)
    qm_ref[...] = wide[pl.ds(o_mid, N_MID, stride=R_MID), :].astype(jnp.bfloat16)
    ql_ref[...] = wide[pl.ds(o_long, N_LONG, stride=R_LONG), :].astype(jnp.bfloat16)
    step = N_MID
    for i in range(N_MID // step):
        n = (i + 1) * step
        s = scores_of(qm_ref[pl.ds(i * step, step), :], kvm[:n])
        top, acc = soft(jnp.where(causal(step, n, i * step), s, NEGATIVE), with_ones(kvm[:n]))
        merge(state, pl.ds(o_mid + i * step * R_MID, step, stride=R_MID), top, acc)
    far = own_ref[...]
    s = scores_of(ql_ref[...], far)
    top, acc = soft(jnp.where(causal(N_LONG, N_LONG, 0), s, NEGATIVE), with_ones(far))
    merge(state, pl.ds(o_long, N_LONG, stride=R_LONG), top, acc)


def mid_part(state, qm, o_mid, pos, parts):
    step = N_MID
    ones = jnp.concatenate([with_ones(ref[...]) for _, ref in parts], axis=0)
    for i in range(N_MID // step):
        q = qm[pl.ds(i * step, step), :]
        pieces = []
        for d, ref in parts:
            before = jnp.bitwise_xor(pos, d) < pos
            pieces.append(scores_of(q, ref[...]) + jnp.where(before, 0.0, NEGATIVE))
        top, new = soft(jnp.concatenate(pieces, axis=1), ones)
        merge(state, pl.ds(o_mid + i * step * R_MID, step, stride=R_MID), top, new)


def long_part(state, ql, o_long, row, its_core, ref):
    every = ref[...].reshape(ZS * N_LONG, LANES)
    s = scores_of(ql[...], every)
    z = (lax.broadcasted_iota(jnp.int32, s.shape, 1) // N_LONG + Z_FIRST) % ZS
    before = 2 * z + its_core < row
    top, new = soft(jnp.where(before, s, NEGATIVE), with_ones(every))
    merge(state, pl.ds(o_long, N_LONG, stride=R_LONG), top, new)


def load_rows(src, first, dst, sems):
    count = sems.shape[0]
    part = dst.shape[0] // count
    pairs = [(src.at[pl.ds(first + i * part, part)], dst.at[pl.ds(i * part, part)]) for i in range(count)]
    return fetch(pairs, sems)


def near_kernel(at_ref, state_in, qm, m1, m2, w_hbm, state, w_ref, w_sems):
    loads = load_rows(w_hbm, 0, w_ref, w_sems)
    o_mid, _ = own_offsets(at_ref)
    mid_part(state, qm, o_mid, lax.rem(lax.axis_index("row"), MID_ROWS), ((1, m1), (2, m2)))
    for load in loads:
        load.wait()


def same_kernel(at_ref, state_in, qm, m3, ql, same, state):
    o_mid, o_long = own_offsets(at_ref)
    row = lax.axis_index("row")
    mid_part(state, qm, o_mid, lax.rem(row, MID_ROWS), ((3, m3),))
    long_part(state, ql, o_long, row, lax.rem(row, 2), same)


def last_kernel(at_ref, state_in, ql, other, w_hbm, out_ref, state, w_ref, w_sems):
    loads = load_rows(w_hbm, w_hbm.shape[0] - w_ref.shape[0], w_ref, w_sems)
    _, o_long = own_offsets(at_ref)
    row = lax.axis_index("row")
    long_part(state, ql, o_long, row, 1 - lax.rem(row, 2), other)
    low = low_lanes(HALF)
    for src in range(HEADS):
        done = []
        for half in range(2):
            a = state[pl.ds(src * BLOCK + half * HALF, HALF), :]
            done.append(a / a[:, :1])
        out_ref[slot(src)] = jnp.where(low, pltpu.roll(done[0], HD, 1), done[1]).astype(jnp.bfloat16)
    for load in loads:
        load.wait()


def project_kernel(got_ref, w0_ref, w1_ref, out_hbm, combined, tiles, sems):
    count, _, tile = tiles.shape
    for pair in range(HEADS // 2):
        a, b = got_ref[slot(2 * pair)], got_ref[slot(2 * pair + 1)]
        cols = pl.ds(pair * LANES, LANES)
        combined[:HALF, cols] = jnp.concatenate([a[:, :HD], b[:, :HD]], axis=1)
        combined[HALF:, cols] = jnp.concatenate([a[:, HD:], b[:, HD:]], axis=1)
    cut = w0_ref.shape[0]
    first, second = combined[:, :cut], combined[:, cut:]
    copies = []
    for i in range(count):
        cols = pl.ds(i * tile, tile)
        total = jnp.dot(first, w0_ref[:, cols], preferred_element_type=jnp.float32)
        total += jnp.dot(second, w1_ref[:, cols], preferred_element_type=jnp.float32)
        tiles[i] = total.astype(jnp.bfloat16)
        copies.append(pltpu.make_async_copy(tiles.at[i], out_hbm.at[:, cols], sems.at[i]))
        copies[-1].start()
    for copy in copies:
        copy.wait()


def xor_rows(x, d):
    return lax.ppermute(x, "row", [(i, i ^ d) for i in range(ROWS)])


CORES = [[2 * ((p + Z_FIRST) % ZS) + c for p in range(ZS)] for c in range(2)]
COLS = [[(p + COL_FIRST) % HEADS for p in range(HEADS)]]
bar = lax.optimization_barrier


def shards(queries, keys, values, mid_offsets, long_offsets, out_weight):
    f32, s32, bf16 = jnp.float32, jnp.int32, jnp.bfloat16
    width = queries.shape[1]
    depth, wide_out = out_weight.shape
    chunks = 4
    sent = call(
        pack_kernel,
        shape(HEADS, PACKED + NOTE, LANES),
        [HB] * 5,
        scratch=[pltpu.SMEM((HEADS,), s32)] * 2
        + [pltpu.VMEM((BLOCK, width), bf16)] * 3
        + [pltpu.VMEM((HEADS, PACKED + NOTE, LANES), bf16), DMA((2,)), DMA((chunks, 3)), DMA((chunks + 1,))],
        moved=1 << 20,
        out_specs=HB,
        limit=VMEM_MOST,
    )(mid_offsets, long_offsets, queries, keys, values)
    got = lax.all_to_all(sent, "col", 0, 0, axis_index_groups=COLS)
    kv_mid, own, at, far = call(
        select_kernel,
        (
            shape(N_MID, LANES),
            shape(N_LONG, LANES),
            shape(NOTE, LANES, dtype=f32),
            shape(ROWS // 2, N_LONG, LANES),
        ),
        [VM],
        scratch=[pltpu.VMEM((SEG, LANES), f32)],
        moved=1 << 20,
    )(got)
    m1 = xor_rows(kv_mid, 1)
    m2 = xor_rows(kv_mid, 2)
    same = lax.all_to_all(far, "row", 0, 0, axis_index_groups=CORES)
    state, q_mid, q_long = call(
        short_kernel,
        (shape(SEG, LANES, dtype=f32), shape(N_MID, LANES), shape(N_LONG, LANES)),
        [VM] * 4,
        scratch=[pltpu.VMEM((SEG, LANES), bf16)] * 2 + [pltpu.VMEM((SEG, LANES), f32)],
        flops=4 * SEG * SEG * LANES,
        moved=3 << 20,
        exps=SEG * SEG // 2,
    )(at, got, kv_mid, own)
    m1, m2, state = bar((m1, m2, state))
    m3 = xor_rows(m2, 1)
    early = depth * 3 // 8
    state, weight0 = call(
        near_kernel,
        (shape(SEG, LANES, dtype=f32), shape(early, wide_out)),
        [VM] * 5 + [HB],
        scratch=[DMA((1,))],
        flops=32 * 4 * N_MID * SEG * LANES,
        moved=2 << 20,
        exps=N_MID * SEG,
        aliases={1: 0},
        limit=VMEM_NEAR,
    )(at, state, q_mid, m1, m2, out_weight)
    same, m3, state = bar((same, m3, state))
    other = xor_rows(same, 1)
    state = call(
        same_kernel,
        shape(SEG, LANES, dtype=f32),
        [VM] * 6,
        flops=4 * N_MID * SEG * LANES,
        moved=2 << 20,
        exps=N_MID * SEG,
        aliases={1: 0},
    )(at, state, q_mid, m3, q_long, same)
    tile = 512
    count = wide_out // tile
    back, _, weight = call(
        last_kernel,
        (shape(HEADS, HALF, LANES), shape(SEG, LANES, dtype=f32), shape(depth - early, wide_out)),
        [VM] * 4 + [HB],
        scratch=[DMA((1,))],
        flops=4 * N_LONG * SEG * LANES,
        moved=4 << 20,
        exps=N_LONG * SEG,
        aliases={1: 1},
        limit=VMEM_LAST,
    )(at, state, q_long, other, out_weight)
    return call(
        project_kernel,
        shape(BLOCK, wide_out),
        [VM, VM, VM],
        scratch=[
            pltpu.VMEM((BLOCK, depth), bf16),
            pltpu.VMEM((count, BLOCK, tile), bf16),
            DMA((count,)),
        ],
        flops=2 * BLOCK * depth * wide_out,
        moved=2 * depth * wide_out,
        out_specs=HB,
    )(lax.all_to_all(back, "col", 0, 0, axis_index_groups=COLS), weight0, weight)


def solution(mesh):
    split = P(("row", "col"), None)
    return jax.shard_map(
        shards,
        mesh=mesh,
        in_specs=(split, split, split, P(), P(), P()),
        out_specs=split,
        check_vma=False,
    )
```

```python
import functools

import jax
import jax.numpy as jnp
from jax import lax
from jax.experimental import pallas as pl
from jax.experimental.pallas import tpu as pltpu
from jax.sharding import PartitionSpec as P

R_MID = 4
R_LONG = 16
HEADS = 16
HD = 64
LANES = 128
BLOCK = 128
SEG = 2048
HALF = BLOCK // 2
PACKED = BLOCK + HALF
NOTE = 16
ROWS = 16
MID_ROWS = 4
ZS = ROWS // 2
Z_FIRST = 5
COL_FIRST = 14
N_MID = SEG // R_MID
N_LONG = SEG // R_LONG
NEGATIVE = -1e30
SCALE = 0.125 * 1.4426950408889634
VMEM_LIMIT = 20 * 1024 * 1024
VMEM_LAST = 47 * 1024 * 1024
VMEM_NEAR = 49 * 1024 * 1024
VMEM_MOST = 60 * 1024 * 1024

VM = pl.BlockSpec(memory_space=pltpu.VMEM)
HB = pl.BlockSpec(memory_space=pl.ANY)
DMA = pltpu.SemaphoreType.DMA


def call(
    kernel, out_shape, in_specs, scratch=(), flops=0, moved=0, exps=0, out_specs=None, aliases=None, limit=VMEM_LIMIT
):
    return pl.pallas_call(
        kernel,
        out_shape=out_shape,
        in_specs=in_specs,
        out_specs=jax.tree.map(lambda _: VM, out_shape) if out_specs is None else out_specs,
        scratch_shapes=list(scratch),
        input_output_aliases=aliases or {},
        compiler_params=pltpu.CompilerParams(vmem_limit_bytes=limit),
        cost_estimate=pl.CostEstimate(flops=flops, bytes_accessed=moved, transcendentals=exps),
    )


def shape(*dims, dtype=jnp.bfloat16):
    return jax.ShapeDtypeStruct(dims, dtype)


def low_lanes(rows):
    return lax.broadcasted_iota(jnp.int32, (rows, LANES), 1) < HD


def fetch(pairs, sems):
    copies = [pltpu.make_async_copy(src, dst, sems.at[i]) for i, (src, dst) in enumerate(pairs)]
    for copy in copies:
        copy.start()
    return copies


def slot(col):
    return (col - COL_FIRST) % HEADS


def pack_kernel(
    mid_hbm, long_hbm, q_hbm, k_hbm, v_hbm, out_hbm,
    mid_ref, long_ref, q_ref, k_ref, v_ref, out_ref, at_sems, in_sems, out_sems,
):
    notes = fetch([(mid_hbm, mid_ref), (long_hbm, long_ref)], at_sems)
    chunks = in_sems.shape[0]
    heads = HEADS // chunks
    loads, stores = [], []
    for i in range(chunks):
        cols = pl.ds(i * heads * HD, heads * HD)
        pairs = [(src.at[:, cols], dst.at[:, cols]) for src, dst in ((k_hbm, k_ref), (v_hbm, v_ref), (q_hbm, q_ref))]
        loads.append(fetch(pairs, in_sems.at[i]))
    for copy in notes:
        copy.wait()
    for i in range(chunks):
        for copy in loads[i]:
            copy.wait()
        for head in range(i * heads, i * heads + heads):
            cols = pl.ds(head // 2 * LANES, LANES)
            lanes = slice(head % 2 * HD, head % 2 * HD + HD)
            q = q_ref[:, cols][:, lanes]
            out_ref[slot(head), :BLOCK] = jnp.concatenate([k_ref[:, cols][:, lanes], v_ref[:, cols][:, lanes]], axis=1)
            out_ref[slot(head), BLOCK:PACKED] = jnp.concatenate([q[:HALF], q[HALF:]], axis=1)
            note = jnp.where(low_lanes(NOTE), mid_ref[head].astype(jnp.float32), long_ref[head].astype(jnp.float32))
            out_ref[slot(head), PACKED:] = note.astype(jnp.bfloat16)
        slots = sorted(slot(head) for head in range(i * heads, i * heads + heads))
        runs = [[at for at in slots if at <= slots[0] + heads], [at for at in slots if at > slots[0] + heads]]
        for run in runs:
            if run:
                done = pl.ds(run[0], len(run))
                stores.append(pltpu.make_async_copy(out_ref.at[done], out_hbm.at[done], out_sems.at[len(stores)]))
                stores[-1].start()
    for copy in stores:
        copy.wait()


def select_kernel(got_ref, kvm_ref, own_ref, at_ref, far_ref, wide):
    at_ref[...] = got_ref[0, PACKED:].astype(jnp.float32)
    o_mid, o_long = own_offsets(at_ref)
    for src in range(HEADS):
        wide[pl.ds(src * BLOCK, BLOCK), :] = got_ref[slot(src), :BLOCK].astype(jnp.float32)
    far = wide[pl.ds(o_long, N_LONG, stride=R_LONG), :].astype(jnp.bfloat16)
    own_ref[...] = far
    for z in range(ROWS // 2):
        far_ref[z] = far
    kvm_ref[...] = wide[pl.ds(o_mid, N_MID, stride=R_MID), :].astype(jnp.bfloat16)


def own_offsets(at_ref):
    lane = lax.broadcasted_iota(jnp.int32, at_ref.shape, 1)
    at = at_ref[...].astype(jnp.int32)
    return [jnp.max(jnp.where(lane == where, at, 0)) for where in (0, LANES - 1)]


def scores_of(q, kv):
    return lax.dot_general(q, kv, (((1,), (1,)), ((), ())), preferred_element_type=jnp.float32)


def with_ones(kv):
    return jnp.where(low_lanes(kv.shape[0]), jnp.ones_like(kv), kv)


def soft(s, kv1):
    top = jnp.max(s, axis=1, keepdims=True)
    w = jnp.exp2((s - top) * SCALE).astype(jnp.bfloat16)
    return top, jnp.dot(w, kv1, preferred_element_type=jnp.float32)


def state_of(top, acc):
    lane = lax.broadcasted_iota(jnp.int32, acc.shape, 1)
    return jnp.where((lane >= HD // 2) & (lane < HD), top, acc)


def merge(state, rows, new_top, new_acc):
    old = state[rows, :]
    old_top = old[:, HD // 2 : HD // 2 + 1]
    best = jnp.maximum(old_top, new_top)
    acc = old * jnp.exp2((old_top - best) * SCALE) + new_acc * jnp.exp2((new_top - best) * SCALE)
    state[rows, :] = state_of(best, acc)


def causal(rows, cols, first):
    at = lax.broadcasted_iota(jnp.int32, (rows, cols), 0) + first
    return lax.broadcasted_iota(jnp.int32, (rows, cols), 1) <= at


def short_kernel(at_ref, got_ref, kvm, own_ref, state, qm_ref, ql_ref, kv_buf, one_buf, wide):
    for src in range(HEADS):
        rows = pl.ds(src * BLOCK, BLOCK)
        kv = got_ref[slot(src), :BLOCK]
        kv_buf[rows, :] = kv
        one_buf[rows, :] = with_ones(kv)
    blocks = 4
    step = blocks * BLOCK
    visible = causal(step, step, 0)
    low = low_lanes(HALF)
    zero = jnp.zeros((HALF, LANES), jnp.bfloat16)
    for i in range(SEG // step):
        parts = []
        for src in range(blocks * i, blocks * i + blocks):
            packed = got_ref[slot(src), BLOCK:PACKED]
            parts.append(jnp.where(low, packed, zero))
            parts.append(jnp.where(low, jnp.concatenate([packed[:, HD:], packed[:, :HD]], axis=1), zero))
        q = jnp.concatenate(parts, axis=0)
        rows = pl.ds(i * step, step)
        wide[rows, :] = q.astype(jnp.float32)
        n = (i + 1) * step
        s = scores_of(q, kv_buf[rows, :])
        s = jnp.where(visible, s, NEGATIVE)
        if i:
            s = jnp.concatenate([scores_of(q, kv_buf[pl.ds(0, i * step), :]), s], axis=1)
        state[rows, :] = state_of(*soft(s, one_buf[pl.ds(0, n), :]))
    o_mid, o_long = own_offsets(at_ref)
    qm_ref[...] = wide[pl.ds(o_mid, N_MID, stride=R_MID), :].astype(jnp.bfloat16)
    ql_ref[...] = wide[pl.ds(o_long, N_LONG, stride=R_LONG), :].astype(jnp.bfloat16)
    step = N_MID
    for i in range(N_MID // step):
        n = (i + 1) * step
        s = scores_of(qm_ref[pl.ds(i * step, step), :], kvm[:n])
        top, acc = soft(jnp.where(causal(step, n, i * step), s, NEGATIVE), with_ones(kvm[:n]))
        merge(state, pl.ds(o_mid + i * step * R_MID, step, stride=R_MID), top, acc)
    far = own_ref[...]
    s = scores_of(ql_ref[...], far)
    top, acc = soft(jnp.where(causal(N_LONG, N_LONG, 0), s, NEGATIVE), with_ones(far))
    merge(state, pl.ds(o_long, N_LONG, stride=R_LONG), top, acc)


def mid_part(state, qm, o_mid, pos, parts):
    step = N_MID
    ones = jnp.concatenate([with_ones(ref[...]) for _, ref in parts], axis=0)
    for i in range(N_MID // step):
        q = qm[pl.ds(i * step, step), :]
        pieces = []
        for d, ref in parts:
            before = jnp.bitwise_xor(pos, d) < pos
            pieces.append(scores_of(q, ref[...]) + jnp.where(before, 0.0, NEGATIVE))
        top, new = soft(jnp.concatenate(pieces, axis=1), ones)
        merge(state, pl.ds(o_mid + i * step * R_MID, step, stride=R_MID), top, new)


def long_part(state, ql, o_long, row, its_core, ref):
    every = ref[...].reshape(ZS * N_LONG, LANES)
    s = scores_of(ql[...], every)
    z = (lax.broadcasted_iota(jnp.int32, s.shape, 1) // N_LONG + Z_FIRST) % ZS
    before = 2 * z + its_core < row
    top, new = soft(jnp.where(before, s, NEGATIVE), with_ones(every))
    merge(state, pl.ds(o_long, N_LONG, stride=R_LONG), top, new)


def load_rows(src, first, dst, sems):
    count = sems.shape[0]
    part = dst.shape[0] // count
    pairs = [(src.at[pl.ds(first + i * part, part)], dst.at[pl.ds(i * part, part)]) for i in range(count)]
    return fetch(pairs, sems)


def near_kernel(at_ref, state_in, qm, m1, m2, w_hbm, state, w_ref, w_sems):
    loads = load_rows(w_hbm, 0, w_ref, w_sems)
    o_mid, _ = own_offsets(at_ref)
    mid_part(state, qm, o_mid, lax.rem(lax.axis_index("row"), MID_ROWS), ((1, m1), (2, m2)))
    for load in loads:
        load.wait()


def same_kernel(at_ref, state_in, qm, m3, ql, same, state):
    o_mid, o_long = own_offsets(at_ref)
    row = lax.axis_index("row")
    mid_part(state, qm, o_mid, lax.rem(row, MID_ROWS), ((3, m3),))
    long_part(state, ql, o_long, row, lax.rem(row, 2), same)


def last_kernel(at_ref, state_in, ql, other, w_hbm, out_ref, state, w_ref, w_sems):
    loads = load_rows(w_hbm, w_hbm.shape[0] - w_ref.shape[0], w_ref, w_sems)
    _, o_long = own_offsets(at_ref)
    row = lax.axis_index("row")
    long_part(state, ql, o_long, row, 1 - lax.rem(row, 2), other)
    low = low_lanes(HALF)
    for src in range(HEADS):
        done = []
        for half in range(2):
            a = state[pl.ds(src * BLOCK + half * HALF, HALF), :]
            done.append(a / a[:, :1])
        out_ref[slot(src)] = jnp.where(low, pltpu.roll(done[0], HD, 1), done[1]).astype(jnp.bfloat16)
    for load in loads:
        load.wait()


def project_kernel(got_ref, w0_ref, w1_ref, out_hbm, combined, tiles, sems):
    count, _, tile = tiles.shape
    for pair in range(HEADS // 2):
        a, b = got_ref[slot(2 * pair)], got_ref[slot(2 * pair + 1)]
        cols = pl.ds(pair * LANES, LANES)
        combined[:HALF, cols] = jnp.concatenate([a[:, :HD], b[:, :HD]], axis=1)
        combined[HALF:, cols] = jnp.concatenate([a[:, HD:], b[:, HD:]], axis=1)
    cut = w0_ref.shape[0]
    first, second = combined[:, :cut], combined[:, cut:]
    copies = []
    for i in range(count):
        cols = pl.ds(i * tile, tile)
        total = jnp.dot(first, w0_ref[:, cols], preferred_element_type=jnp.float32)
        total += jnp.dot(second, w1_ref[:, cols], preferred_element_type=jnp.float32)
        tiles[i] = total.astype(jnp.bfloat16)
        copies.append(pltpu.make_async_copy(tiles.at[i], out_hbm.at[:, cols], sems.at[i]))
        copies[-1].start()
    for copy in copies:
        copy.wait()


def xor_rows(x, d):
    return lax.ppermute(x, "row", [(i, i ^ d) for i in range(ROWS)])


CORES = [[2 * ((p + Z_FIRST) % ZS) + c for p in range(ZS)] for c in range(2)]
COLS = [[(p + COL_FIRST) % HEADS for p in range(HEADS)]]
bar = lax.optimization_barrier


def shards(queries, keys, values, mid_offsets, long_offsets, out_weight):
    f32, s32, bf16 = jnp.float32, jnp.int32, jnp.bfloat16
    width = queries.shape[1]
    depth, wide_out = out_weight.shape
    chunks = 4
    sent = call(
        pack_kernel,
        shape(HEADS, PACKED + NOTE, LANES),
        [HB] * 5,
        scratch=[pltpu.SMEM((HEADS,), s32)] * 2
        + [pltpu.VMEM((BLOCK, width), bf16)] * 3
        + [pltpu.VMEM((HEADS, PACKED + NOTE, LANES), bf16), DMA((2,)), DMA((chunks, 3)), DMA((chunks + 1,))],
        moved=1 << 20,
        out_specs=HB,
        limit=VMEM_MOST,
    )(mid_offsets, long_offsets, queries, keys, values)
    got = lax.all_to_all(sent, "col", 0, 0, axis_index_groups=COLS)
    kv_mid, own, at, far = call(
        select_kernel,
        (
            shape(N_MID, LANES),
            shape(N_LONG, LANES),
            shape(NOTE, LANES, dtype=f32),
            shape(ROWS // 2, N_LONG, LANES),
        ),
        [VM],
        scratch=[pltpu.VMEM((SEG, LANES), f32)],
        moved=1 << 20,
    )(got)
    m1 = xor_rows(kv_mid, 1)
    m2 = xor_rows(kv_mid, 2)
    same = lax.all_to_all(far, "row", 0, 0, axis_index_groups=CORES)
    state, q_mid, q_long = call(
        short_kernel,
        (shape(SEG, LANES, dtype=f32), shape(N_MID, LANES), shape(N_LONG, LANES)),
        [VM] * 4,
        scratch=[pltpu.VMEM((SEG, LANES), bf16)] * 2 + [pltpu.VMEM((SEG, LANES), f32)],
        flops=4 * SEG * SEG * LANES,
        moved=3 << 20,
        exps=SEG * SEG // 2,
    )(at, got, kv_mid, own)
    m1, m2, state = bar((m1, m2, state))
    m3 = xor_rows(m2, 1)
    early = depth * 3 // 8
    state, weight0 = call(
        near_kernel,
        (shape(SEG, LANES, dtype=f32), shape(early, wide_out)),
        [VM] * 5 + [HB],
        scratch=[DMA((1,))],
        flops=32 * 4 * N_MID * SEG * LANES,
        moved=2 << 20,
        exps=N_MID * SEG,
        aliases={1: 0},
        limit=VMEM_NEAR,
    )(at, state, q_mid, m1, m2, out_weight)
    same, m3, state = bar((same, m3, state))
    other = xor_rows(same, 1)
    state = call(
        same_kernel,
        shape(SEG, LANES, dtype=f32),
        [VM] * 6,
        flops=4 * N_MID * SEG * LANES,
        moved=2 << 20,
        exps=N_MID * SEG,
        aliases={1: 0},
    )(at, state, q_mid, m3, q_long, same)
    tile = 512
    count = wide_out // tile
    back, _, weight = call(
        last_kernel,
        (shape(HEADS, HALF, LANES), shape(SEG, LANES, dtype=f32), shape(depth - early, wide_out)),
        [VM] * 4 + [HB],
        scratch=[DMA((1,))],
        flops=4 * N_LONG * SEG * LANES,
        moved=4 << 20,
        exps=N_LONG * SEG,
        aliases={1: 1},
        limit=VMEM_LAST,
    )(at, state, q_long, other, out_weight)
    return call(
        project_kernel,
        shape(BLOCK, wide_out),
        [VM, VM, VM],
        scratch=[
            pltpu.VMEM((BLOCK, depth), bf16),
            pltpu.VMEM((count, BLOCK, tile), bf16),
            DMA((count,)),
        ],
        flops=2 * BLOCK * depth * wide_out,
        moved=2 * depth * wide_out,
        out_specs=HB,
    )(lax.all_to_all(back, "col", 0, 0, axis_index_groups=COLS), weight0, weight)


def solution(mesh):
    split = P(("row", "col"), None)
    return jax.shard_map(
        shards,
        mesh=mesh,
        in_specs=(split, split, split, P(), P(), P()),
        out_specs=split,
        check_vma=False,
    )
```
